512 devices in a mesh: space: 128 (over z, x, core), level: 4 (over y).
Axes of the slice: x: 4, y: 4, z: 16, core: 2. Of those that a mesh axis runs over, the one named last changes fastest.
Arguments:
- rhs: float32 [64, 4, 65536], P(None, None, ('space', 'level')), may hold values from -6 to 6
- fine_diag: bfloat16 [64, 64, 65536], P(None, None, ('space', 'level'))
- fine_off: bfloat16 [64, 2, 64, 65536], P(None, None, None, ('space', 'level')), may hold values from -0.375 to 0.375
- fine_cols: int32 [2, 65536], P(None, ('space', 'level')), may hold values from 0 to 65535, as said below
- aggregates: int32 [65536], P(('space', 'level')), may hold values from 0 to 16383, as said below
- coarse_diag: bfloat16 [64, 64, 16384], P(None, None, 'space')
- coarse_off: bfloat16 [64, 2, 64, 16384], P('level', None, None, 'space'), may hold values from -1.5 to 1.5
- coarse_cols: int32 [2, 16384], P(None, 'space'), may hold values from 0 to 16383, as said below
Outputs:
- solution: float32 [64, 4, 65536], P(None, None, ('space', 'level'))
The draws below stay inside these ranges and needn't reach their ends.
Inputs may be any that keep to these rules, and one draw needn't show every extreme that they name: `fine_cols`: row 0 names for each cell another cell at most 64 cells before it (after it where none lies before), row 1 one at most 64 cells after it (before it where none lies after); every device's rows reach the distance 64. `coarse_cols`: as fine_cols, over coarse blocks with the distance 64. `aggregates`: cell c belongs to a coarse block of section c // 512, that is to a block numbered from (c // 512) * 128 up; every coarse block holds exactly 4 cells.
All inputs are finite; a program needn't handle non-finite values.
Results may differ from the reference program's by a relative error of at most 0.0085.
Values may be sent and summed in bfloat16 or wider, within the bound.
A program may use at most 64 MiB of HBM per device.

```python
import math
import jax
import jax.numpy as jnp
from jax import lax

S = 64
R = 4
CELL_DEV = 128
KF = 2
KC = 2
AGG = 4
PRE = 2
POST = 1
CSWEEPS = 3
CELLS = 65536
HALO = 64
CSEC = 128
CHALO = 64
COARSE = 16384


def reach_table(key, total_count, reach_width):
    first_key, second_key = jax.random.split(key)
    positions = jnp.arange(total_count, dtype=jnp.int32)
    backward = jax.random.randint(first_key, (total_count,), 1, reach_width + 1, dtype=jnp.int32)
    forward = jax.random.randint(second_key, (total_count,), 1, reach_width + 1, dtype=jnp.int32)
    backward = jnp.where(positions % reach_width == 0, reach_width, backward)
    forward = jnp.where(positions % reach_width == 1 % reach_width, reach_width, forward)
    left_col = positions - backward
    left_col = jnp.where(left_col < 0, positions + backward, left_col)
    right_col = positions + forward
    right_col = jnp.where(right_col >= total_count, positions - forward, right_col)
    return jnp.stack([left_col, right_col]).astype(jnp.int32)


def draw_fine_cols(key, part):
    key = jax.random.fold_in(key, 3)
    return reach_table(key, CELLS, HALO)


def draw_coarse_cols(key, part):
    key = jax.random.fold_in(key, 4)
    return reach_table(key, COARSE, CHALO)


def draw_aggregates(key, part):
    key = jax.random.fold_in(key, 5)
    sections = COARSE // CSEC
    group_cells = CSEC * AGG
    section_keys = jax.random.split(key, sections)
    orders = jax.vmap(lambda one_key: jax.random.permutation(one_key, group_cells))(section_keys)
    labels = orders.astype(jnp.int32) // AGG + jnp.arange(sections, dtype=jnp.int32)[:, None] * CSEC
    return labels.reshape(-1).astype(jnp.int32)


def draw_fine_diag(key, part):
    key = jax.random.fold_in(key, 1)
    first_key, second_key = jax.random.split(key)
    identity = jnp.eye(S, dtype=jnp.float32)[:, :, None]
    pivots = jax.random.uniform(first_key, (S, CELLS), jnp.float32, 1.5, 3.0)
    noise = jax.random.normal(second_key, (S, S, CELLS), jnp.float32) * (0.5 / math.sqrt(S))
    return (identity * pivots[:, None, :] + (1.0 - identity) * noise).astype(jnp.bfloat16)


def draw_coarse_diag(key, part):
    key = jax.random.fold_in(key, 2)
    first_key, second_key = jax.random.split(key)
    identity = jnp.eye(S, dtype=jnp.float32)[:, :, None]
    pivots = jax.random.uniform(first_key, (S, COARSE), jnp.float32, 1.5, 3.0)
    noise = jax.random.normal(second_key, (S, S, COARSE), jnp.float32) * (0.5 / math.sqrt(S))
    return (identity * pivots[:, None, :] + (1.0 - identity) * noise).astype(jnp.bfloat16)


def block_levels(key, extent, cuts, smallest, largest):
    gain = 1.0
    for position, shards_of in cuts:
        steps = jax.random.uniform(jax.random.fold_in(jax.random.fold_in(key, 6), position), (shards_of,), jnp.float32, smallest / len(cuts), largest / len(cuts))
        gain = gain * jnp.repeat(jnp.exp(steps), extent[position] // shards_of).reshape((-1,) + (1,) * (len(extent) - 1 - position))
    return gain


def gaussian(key, shape, width, most, cuts=(), held_as=jnp.bfloat16):
    gain = block_levels(key, shape, cuts, -0.22, 0.18) if cuts else 1.0
    array = jax.random.normal(key, shape, jnp.float32) * width * gain
    return jnp.minimum(jnp.maximum(array, -most), most).astype(held_as)


def setup_inputs(seed: int = 0) -> dict:
    key_of = jax.random.split(jax.random.key(seed), 9)
    return {
        "rhs": gaussian(key_of[0], (S, R, CELLS), 1.0, 6.0, ((2, 512),), jnp.float32),
        "fine_diag": draw_fine_diag(jax.random.fold_in(key_of[8], 71), 0),
        "fine_off": gaussian(key_of[2], (S, KF, S, CELLS), (0.5 / S ** 0.5), 0.375, ((3, 512),)),
        "fine_cols": draw_fine_cols(jax.random.fold_in(key_of[8], 71), 0),
        "aggregates": draw_aggregates(jax.random.fold_in(key_of[8], 71), 0),
        "coarse_diag": draw_coarse_diag(jax.random.fold_in(key_of[8], 71), 0),
        "coarse_off": gaussian(key_of[6], (S, KC, S, COARSE), (2.0 / S ** 0.5), 1.5, ((0, 4), (3, 128))),
        "coarse_cols": draw_coarse_cols(jax.random.fold_in(key_of[8], 71), 0),
    }


OMEGA = 0.7


def approx_inverse(diag_blocks):
    order_size = diag_blocks.shape[0]
    identity = jnp.eye(order_size, dtype=jnp.float32)[:, :, None]
    widened = diag_blocks.astype(jnp.float32)
    pivots = jnp.sum(widened * identity, axis=1)
    inverse = (2.0 * identity * pivots[:, None, :] - widened) / (pivots[:, None, :] * pivots[None, :, :])
    return inverse.astype(jnp.bfloat16)


def blockwise(compute, span_width, operands):
    total_count = operands[0].shape[-1] // span_width

    def one_block(block_index):
        first_cell = block_index * span_width
        pieces = [lax.dynamic_slice_in_dim(operand, first_cell, span_width, operand.ndim - 1) for operand in operands]
        return compute(*pieces)

    stacked = lax.map(one_block, jnp.arange(total_count, dtype=jnp.int32))
    moved = jnp.moveaxis(stacked, 0, 2)
    return moved.reshape(moved.shape[0], moved.shape[1], -1)


def operator_apply(field, diag_blocks, off_blocks, columns, span_width):
    rounded = field.astype(jnp.bfloat16)

    def compute(diag_piece, off_piece, column_piece, own_piece):
        neighbours = rounded[:, :, column_piece]
        own_term = jnp.einsum("ijc,jrc->irc", diag_piece.astype(jnp.float32), own_piece.astype(jnp.float32))
        far_term = jnp.einsum("ikjc,jrkc->irc", off_piece.astype(jnp.float32), neighbours.astype(jnp.float32))
        return own_term + far_term

    return blockwise(compute, span_width, [diag_blocks, off_blocks, columns, rounded])


def smoother(field, diag_blocks, span_width):
    rounded = field.astype(jnp.bfloat16)

    def compute(diag_piece, own_piece):
        inverse = approx_inverse(diag_piece)
        return OMEGA * jnp.einsum("ijc,jrc->irc", inverse.astype(jnp.float32), own_piece.astype(jnp.float32))

    return blockwise(compute, span_width, [diag_blocks, rounded])


def reference(rhs, fine_diag, fine_off, fine_cols, aggregates, coarse_diag, coarse_off, coarse_cols):
    iterate = smoother(rhs, fine_diag, CELL_DEV)
    for sweep_index in range(PRE - 1):
        iterate = iterate + smoother(rhs - operator_apply(iterate, fine_diag, fine_off, fine_cols, CELL_DEV), fine_diag, CELL_DEV)
    residual = rhs - operator_apply(iterate, fine_diag, fine_off, fine_cols, CELL_DEV)
    summed = jax.ops.segment_sum(jnp.moveaxis(residual, 2, 0), aggregates, num_segments=COARSE)
    coarse_rhs = jnp.moveaxis(summed, 0, 2)
    correction = smoother(coarse_rhs, coarse_diag, CSEC)
    for sweep_index in range(CSWEEPS - 1):
        shortfall = coarse_rhs - operator_apply(correction, coarse_diag, coarse_off, coarse_cols, CSEC)
        correction = correction + smoother(shortfall, coarse_diag, CSEC)
    iterate = iterate + correction[:, :, aggregates]
    for sweep_index in range(POST):
        iterate = iterate + smoother(rhs - operator_apply(iterate, fine_diag, fine_off, fine_cols, CELL_DEV), fine_diag, CELL_DEV)
    return iterate
```

```python
import functools

import jax
import jax.numpy as jnp
from jax import lax
from jax.experimental import pallas as pl
from jax.experimental.pallas import tpu as pltpu
from jax.sharding import PartitionSpec as P

CSWEEPS = 3
OMEGA = 0.7
S = 64
R = 4
C = 128
HALF = 64
ROWS = 16
MESH = pl.DeviceIdType.MESH
F32 = jnp.float32
BF16 = jnp.bfloat16


def lane_low(rows):
    return lax.broadcasted_iota(jnp.int32, (rows, C), 1) < HALF


def fold_rows(parts):
    sub = lax.broadcasted_iota(jnp.int32, (8, C), 0)
    four = sub < 4
    two = lax.rem(sub, 4) < 2
    one = lax.rem(sub, 2) < 1
    level = [
        jnp.where(four, parts[i], parts[i + 4])
        + pltpu.roll(jnp.where(four, parts[i + 4], parts[i]), 4, 0)
        for i in range(4)
    ]
    level = [
        jnp.where(
            two,
            level[i] + pltpu.roll(level[i], 6, 0),
            level[i + 2] + pltpu.roll(level[i + 2], 2, 0),
        )
        for i in range(2)
    ]
    return jnp.where(
        one,
        level[0] + pltpu.roll(level[0], 7, 0),
        level[1] + pltpu.roll(level[1], 1, 0),
    )


def products(base, terms, start=None):
    sums = [[None] * R for _ in range(8)] if start is None else start
    for load, vector in terms:
        for block in range(S // 16):
            low = block * 16
            pieces = [vector[r, low : low + 16, :] for r in range(R)]
            for i in range(8):
                matrix = load(base + i, low).astype(F32)
                for r in range(R):
                    product = matrix * pieces[r]
                    piece = product[:8] + product[8:]
                    sums[i][r] = piece if sums[i][r] is None else sums[i][r] + piece
    return sums


def diag_load(ref, offset=0):
    return lambda row, low: ref[row + offset, low : low + 16, :]


def off_load(ref, first):
    def load(row, low):
        return jnp.where(
            lane_low(16),
            ref[row, first, low : low + 16, :],
            ref[row, 1 - first, low : low + 16, :],
        )

    return load


def apply_first(count, diag_ref, row_start, off_ref, vector, near, acc):
    def step(block, carry):
        base = block * 8
        sums = products(
            base,
            [(diag_load(diag_ref, row_start), vector), (off_load(off_ref, 1), near)],
        )
        for i in range(8):
            for r in range(R):
                acc[block, i * R + r] = sums[i][r]
        return carry

    lax.fori_loop(0, count // 8, step, 0)


def apply_last(count, off_ref, far, acc, out):
    def step(block, carry):
        start = [[acc[block, i * R + r] for r in range(R)] for i in range(8)]
        sums = products(block * 8, [(off_load(off_ref, 0), far)], start)
        low = pl.multiple_of(block * 8, 8)
        for r in range(R):
            out[r, pl.ds(low, 8), :] = fold_rows([sums[i][r] for i in range(8)])
        return carry

    lax.fori_loop(0, count // 8, step, 0)


def smooth(diag_ref, scale, field, scaled, out):
    for r in range(R):
        scaled[r] = field[r] * scale[...]

    def step(block, carry):
        base = block * 8
        sums = products(base, [(diag_load(diag_ref), scaled)])
        low = pl.multiple_of(base, 8)
        rows = pl.ds(low, 8)
        for r in range(R):
            total = fold_rows([sums[i][r] for i in range(8)])
            out[r, rows, :] = (OMEGA * scale[rows, :]) * (2.0 * field[r, rows, :] - total)
        return carry

    lax.fori_loop(0, S // 8, step, 0)


def pivot_scale(diag_ref, scale):
    sub = lax.broadcasted_iota(jnp.int32, (16, C), 0)

    def step(block, carry):
        low = pl.multiple_of(block * 16, 16)
        total = jnp.zeros((16, C), F32)
        for i in range(16):
            row = diag_ref[low + i, pl.ds(low, 16), :].astype(F32)
            total = jnp.where(sub == i, row, total)
        scale[pl.ds(low, 16), :] = 1.0 / total
        return carry

    lax.fori_loop(0, S // 16, step, 0)


def one_hot(cells, width):
    return (lax.broadcasted_iota(jnp.int32, (width, C), 0) == cells).astype(F32).astype(BF16)


def flat(field):
    return field.reshape(R * S, C)


def split_dot(field, matrix, dims):
    high = field.astype(BF16)
    low = (field - high.astype(F32)).astype(BF16)
    dot = lambda part: lax.dot_general(part, matrix, (dims, ((), ())), preferred_element_type=F32)
    return dot(high) + dot(low)


def kernel(
    sizes,
    rhs_hbm, diag_hbm, off_hbm, cols_ref, agg_ref, cdiag_hbm, coff_hbm, ccols_ref,
    out_ref,
    rhs_in, diag, off, cdiag, coff,
    b, x, q, u, d, xb, near, far, acc, scale, cscale, cb, e,
    hot_near, hot_far, chot_near, chot_far, member,
    send_fine, get_fine, send_coarse, get_coarse,
    send_part, get_part, send_short, get_short,
    load_sem, fine_send, fine_get, coarse_send, coarse_get,
    part_send, part_get, short_send, short_get,
):
    spaces, levels = sizes
    space = lax.axis_index("space")
    level = lax.axis_index("level")
    index = space * levels + level
    count = spaces * levels
    after = lax.rem(index + 1, count)
    before = lax.rem(index + count - 1, count)
    fine_next = (lax.div(after, levels), lax.rem(after, levels))
    fine_last = (lax.div(before, levels), lax.rem(before, levels))
    space_next = (lax.rem(space + 1, spaces), level)
    space_last = (lax.rem(space + spaces - 1, spaces), level)
    peers = [(space, lax.rem(level + k, levels)) for k in range(1, levels)]

    barrier = pltpu.get_barrier_semaphore()
    partners = [fine_next, fine_last, space_next, space_last] + peers
    for partner in partners:
        pl.semaphore_signal(barrier, inc=1, device_id=partner, device_id_type=MESH)

    loads = [
        pltpu.make_async_copy(source, target, load_sem.at[k])
        for k, (source, target) in enumerate(
            [(rhs_hbm, rhs_in), (diag_hbm, diag), (off_hbm, off), (cdiag_hbm, cdiag), (coff_hbm, coff)]
        )
    ]
    for load in loads:
        load.start()

    def remote(source, target, sent, got, device):
        return pltpu.make_async_remote_copy(
            src_ref=source, dst_ref=target, send_sem=sent, recv_sem=got,
            device_id=device, device_id_type=MESH,
        )

    low_lane = lax.broadcasted_iota(jnp.int32, (1, C), 1) < HALF

    def tables(cols, first, near_table, far_table):
        place = cols - first
        own = jnp.where(low_lane, place[1:2], place[0:1])
        reach = jnp.where(low_lane, place[0:1], place[1:2])
        near_table[...] = one_hot(own, C)
        left = jnp.where(reach < 0, reach + HALF, -1)
        right = jnp.where(reach >= C, reach - HALF, -1)
        rim = jnp.maximum(left, right)
        swapped = jnp.where(rim < 0, rim, lax.rem(rim + HALF, C))
        far_table[0, 0:C] = one_hot(rim, C)
        far_table[1, 0:C] = one_hot(swapped, C)
        inner = one_hot(reach, C)
        far_table[0, C:] = inner
        far_table[1, C:] = inner

    tables(cols_ref[...], index * C, hot_near, hot_far)
    tables(ccols_ref[...], space * C, chot_near, chot_far)
    member[...] = one_hot(agg_ref[...] - space * C, C)

    def start_rims(field, sends, gets, send_sems, get_sems, devices):
        rounded = flat(field[...]).astype(BF16)
        xb[...] = rounded
        wide = rounded.astype(F32)
        for r in range(R):
            d[r] = wide[r * S : (r + 1) * S]
        lower, upper = wide[: R * S // 2], wide[R * S // 2 :]
        turned = pltpu.roll(lower, HALF, 1)
        mask = lane_low(R * S // 2)
        sends[0] = jnp.where(mask, turned, upper).astype(BF16)
        sends[1] = jnp.where(mask, upper, turned).astype(BF16)
        copies = [
            remote(sends.at[k], gets.at[k], send_sems.at[k], get_sems.at[k], devices[k])
            for k in range(2)
        ]
        for copy in copies:
            copy.start()
        return copies

    def gather_near(table):
        near[...] = jnp.dot(xb[...], table[...], preferred_element_type=F32).reshape(R, S, C)

    def gather_far(gets, table):
        mask = lane_low(R * S // 2)
        from_left, from_right = gets[0].astype(F32), gets[1].astype(F32)
        half = R * S // 2
        for k in range(2):
            rim = jnp.where(mask, from_left, from_right) if k == 0 else jnp.where(mask, from_right, from_left)
            own = xb[k * half : (k + 1) * half]
            value = jnp.dot(rim.astype(BF16), table[k, 0:C], preferred_element_type=F32) + jnp.dot(
                own, table[k, C:], preferred_element_type=F32
            )
            far[k * R // 2 : (k + 1) * R // 2] = value.reshape(R // 2, S, C)

    waiting = []

    def fine_residual(phase):
        copies = start_rims(
            x, send_fine.at[phase], get_fine.at[phase],
            fine_send.at[phase], fine_get.at[phase], (fine_next, fine_last),
        )
        waiting.extend(copies)
        gather_near(hot_near)
        if phase == 0:
            loads[2].wait()
        apply_first(S, diag, 0, off, d, near, acc)
        for copy in copies:
            copy.wait_recv()
        gather_far(get_fine.at[phase], hot_far)
        apply_last(S, off, far, acc, q)
        q[...] = b[...] - q[...]

    loads[0].wait()
    for r in range(R):
        b[r] = rhs_in[:, r, :]
    loads[1].wait()
    pivot_scale(diag, scale)
    smooth(diag, scale, b, u, x)
    pl.semaphore_wait(barrier, len(partners))

    fine_residual(0)
    smooth(diag, scale, q, u, d)
    x[...] = x[...] + d[...]
    fine_residual(1)

    send_part[...] = split_dot(flat(q[...]), member[...], ((1,), (1,))).astype(BF16)
    parts = [
        remote(send_part, get_part.at[k], part_send.at[k], part_get.at[k], peer)
        for k, peer in enumerate(peers)
    ]
    for copy in parts:
        copy.start()
    waiting.extend(parts)
    loads[3].wait()
    loads[4].wait()
    pivot_scale(cdiag, cscale)
    for copy in parts:
        copy.wait_recv()
    total = send_part[...].astype(F32)
    for k in range(levels - 1):
        total = total + get_part[k].astype(F32)
    cb[...] = total.reshape(R, S, C)

    smooth(cdiag, cscale, cb, u, e)
    row_start = pl.multiple_of(level * ROWS, ROWS)
    for sweep in range(CSWEEPS - 1):
        copies = start_rims(
            e, send_coarse.at[sweep], get_coarse.at[sweep],
            coarse_send.at[sweep], coarse_get.at[sweep], (space_next, space_last),
        )
        waiting.extend(copies)
        gather_near(chot_near)
        apply_first(ROWS, cdiag, row_start, coff, d, near, acc)
        for copy in copies:
            copy.wait_recv()
        gather_far(get_coarse.at[sweep], chot_far)
        apply_last(ROWS, coff, far, acc, q)
        for r in range(R):
            send_short[sweep, r] = (cb[r, pl.ds(row_start, ROWS), :] - q[r, 0:ROWS, :]).astype(BF16)
        copies = [
            remote(
                send_short.at[sweep], get_short.at[sweep, k],
                short_send.at[sweep, k], short_get.at[sweep, k], peer,
            )
            for k, peer in enumerate(peers)
        ]
        for copy in copies:
            copy.start()
        waiting.extend(copies)
        for r in range(R):
            q[r, pl.ds(row_start, ROWS), :] = send_short[sweep, r].astype(F32)
        for k, copy in enumerate(copies):
            copy.wait_recv()
            source = lax.rem(level + levels - (k + 1), levels)
            rows = pl.ds(pl.multiple_of(source * ROWS, ROWS), ROWS)
            for r in range(R):
                q[r, rows, :] = get_short[sweep, k, r].astype(F32)
        smooth(cdiag, cscale, q, u, d)
        e[...] = e[...] + d[...]

    x[...] = x[...] + split_dot(flat(e[...]), member[...], ((1,), (0,))).reshape(R, S, C)
    fine_residual(2)
    smooth(diag, scale, q, u, d)
    out_ref[...] = x[...] + d[...]
    for copy in waiting:
        copy.wait_send()


def local(sizes, rhs, fine_diag, fine_off, fine_cols, aggregates, coarse_diag, coarse_off, coarse_cols):
    levels = sizes[1]
    vmem = pl.BlockSpec(memory_space=pltpu.VMEM)
    hbm = pl.BlockSpec(memory_space=pl.ANY)
    field = pltpu.VMEM((R, S, C), F32)
    dma = pltpu.SemaphoreType.DMA
    half = R * S // 2
    sweeps = CSWEEPS - 1
    result = pl.pallas_call(
        functools.partial(kernel, sizes),
        out_shape=jax.ShapeDtypeStruct((R, S, C), F32),
        in_specs=[hbm, hbm, hbm, vmem, vmem, hbm, hbm, vmem],
        out_specs=vmem,
        scratch_shapes=[
            pltpu.VMEM((S, R, C), F32),
            pltpu.VMEM((S, S, C), BF16),
            pltpu.VMEM((S, 2, S, C), BF16),
            pltpu.VMEM((S, S, C), BF16),
            pltpu.VMEM((ROWS, 2, S, C), BF16),
            field, field, field, field, field,
            pltpu.VMEM((R * S, C), BF16),
            field, field,
            pltpu.VMEM((S // 8, 8 * R, 8, C), F32),
            pltpu.VMEM((S, C), F32),
            pltpu.VMEM((S, C), F32),
            field, field,
            pltpu.VMEM((C, C), BF16),
            pltpu.VMEM((2, 2 * C, C), BF16),
            pltpu.VMEM((C, C), BF16),
            pltpu.VMEM((2, 2 * C, C), BF16),
            pltpu.VMEM((C, C), BF16),
            pltpu.VMEM((3, 2, half, C), BF16),
            pltpu.VMEM((3, 2, half, C), BF16),
            pltpu.VMEM((sweeps, 2, half, C), BF16),
            pltpu.VMEM((sweeps, 2, half, C), BF16),
            pltpu.VMEM((R * S, C), BF16),
            pltpu.VMEM((levels - 1, R * S, C), BF16),
            pltpu.VMEM((sweeps, R, ROWS, C), BF16),
            pltpu.VMEM((sweeps, levels - 1, R, ROWS, C), BF16),
            dma((5,)),
            dma((3, 2)),
            dma((3, 2)),
            dma((sweeps, 2)),
            dma((sweeps, 2)),
            dma((levels - 1,)),
            dma((levels - 1,)),
            dma((sweeps, levels - 1)),
            dma((sweeps, levels - 1)),
        ],
        compiler_params=pltpu.CompilerParams(
            collective_id=0, has_side_effects=True, vmem_limit_bytes=48 * 1024 * 1024
        ),
        name="vcycle",
    )(
        rhs, fine_diag, fine_off, fine_cols, aggregates.reshape(1, C),
        coarse_diag, coarse_off, coarse_cols,
    )
    return result.transpose(1, 0, 2)


def solution(mesh):
    placed = (
        P(None, None, ("space", "level")),
        P(None, None, ("space", "level")),
        P(None, None, None, ("space", "level")),
        P(None, ("space", "level")),
        P(("space", "level")),
        P(None, None, "space"),
        P("level", None, None, "space"),
        P(None, "space"),
    )
    sizes = (mesh.shape["space"], mesh.shape["level"])
    return jax.shard_map(
        functools.partial(local, sizes),
        mesh=mesh,
        in_specs=placed,
        out_specs=P(None, None, ("space", "level")),
        check_vma=False,
    )
```

```python
import functools

import jax
import jax.numpy as jnp
from jax import lax
from jax.experimental import pallas as pl
from jax.experimental.pallas import tpu as pltpu
from jax.sharding import PartitionSpec as P

OMEGA = 0.7
S = 64
R = 4
GROUPS = 2
PAIR = R // GROUPS
C = 128
HALF = 64
ROWS = 16
SPAN = PAIR // 2 * S
RIMS = 5
FINE, COARSE = 0, 1
MESH = pl.DeviceIdType.MESH
F32 = jnp.float32
BF16 = jnp.bfloat16


def lane_low(rows):
    return lax.broadcasted_iota(jnp.int32, (rows, C), 1) < HALF


def fold_rows(parts):
    sub = lax.broadcasted_iota(jnp.int32, (8, C), 0)
    four = sub < 4
    two = lax.rem(sub, 4) < 2
    one = lax.rem(sub, 2) < 1
    level = [
        jnp.where(four, parts[i], parts[i + 4])
        + pltpu.roll(jnp.where(four, parts[i + 4], parts[i]), 4, 0)
        for i in range(4)
    ]
    level = [
        jnp.where(
            two,
            level[i] + pltpu.roll(level[i], 6, 0),
            level[i + 2] + pltpu.roll(level[i + 2], 2, 0),
        )
        for i in range(2)
    ]
    return jnp.where(
        one,
        level[0] + pltpu.roll(level[0], 7, 0),
        level[1] + pltpu.roll(level[1], 1, 0),
    )


def products(terms, start=None):
    sums = [[None] * PAIR for _ in range(8)] if start is None else start
    for load, vector in terms:
        for low in range(0, S, 8):
            pieces = [vector(r, low) for r in range(PAIR)]
            for i in range(8):
                matrix = load(i, low)
                for r in range(PAIR):
                    piece = matrix * pieces[r]
                    sums[i][r] = piece if sums[i][r] is None else sums[i][r] + piece
    return sums


def kernel(
    sizes,
    rhs_hbm, diag_hbm, off_hbm, cols_hbm, agg_hbm, cdiag_hbm, coff_hbm, ccols_hbm,
    out_hbm,
    cols_ref, agg_ref, ccols_ref, rhs_in, diag_in, off_in, diag, off_near, off_far, scale, fixed, field, q, u, xb, xw, near, far, acc,
    hot_near, hot_far, member,
    send_rim, get_rim, send_part, get_part, send_short, get_short,
    load_sem, save_sem, rim_send, rim_get, part_send, part_get, short_send, short_get,
):
    spaces, levels = sizes
    space = lax.axis_index("space")
    level = lax.axis_index("level")
    index = space * levels + level
    count = spaces * levels
    after = lax.rem(index + 1, count)
    before = lax.rem(index + count - 1, count)
    fine_next = (lax.div(after, levels), lax.rem(after, levels))
    fine_last = (lax.div(before, levels), lax.rem(before, levels))
    space_next = (lax.rem(space + 1, spaces), level)
    space_last = (lax.rem(space + spaces - 1, spaces), level)
    peers = [(space, lax.rem(level + k, levels)) for k in range(1, levels)]

    barrier = pltpu.get_barrier_semaphore()
    partners = [fine_next, fine_last, space_next, space_last] + peers
    for partner in partners:
        pl.semaphore_signal(barrier, inc=1, device_id=partner, device_id_type=MESH)

    def load(k, source, target):
        return pltpu.make_async_copy(source, target, load_sem.at[k])

    half = S // 2
    load_diag = [
        load(k, diag_hbm.at[k * half : (k + 1) * half], diag_in.at[FINE, k * half : (k + 1) * half])
        for k in range(2)
    ]
    load_rhs = load(2, rhs_hbm, rhs_in)
    load_cols = load(3, cols_hbm, cols_ref)
    load_off = [
        load(4 + k, off_hbm.at[k * half : (k + 1) * half], off_in.at[k * half : (k + 1) * half])
        for k in range(2)
    ]
    load_coarse = [
        load(6, agg_hbm, agg_ref),
        load(7, ccols_hbm, ccols_ref),
        load(8, cdiag_hbm, diag_in.at[COARSE]),
        load(9, coff_hbm, off_in.at[S : S + ROWS]),
    ]
    for copy in load_diag + [load_rhs, load_cols] + load_off + load_coarse:
        copy.start()

    def remote(source, target, sent, got, device):
        return pltpu.make_async_remote_copy(
            src_ref=source, dst_ref=target, send_sem=sent, recv_sem=got,
            device_id=device, device_id_type=MESH,
        )

    def rim_copies(rim, group, kind):
        targets = (fine_next, fine_last) if kind == FINE else (space_next, space_last)
        return [
            remote(
                send_rim.at[rim, group, k], get_rim.at[rim, group, k],
                rim_send.at[rim, group, k], rim_get.at[rim, group, k], targets[k],
            )
            for k in range(2)
        ]

    def part_copies(group):
        return [
            remote(
                send_part.at[group], get_part.at[group, k],
                part_send.at[group, k], part_get.at[group, k], peer,
            )
            for k, peer in enumerate(peers)
        ]

    def short_copies(sweep, group):
        return [
            remote(
                send_short.at[sweep, group], get_short.at[sweep, group, k],
                short_send.at[sweep, group, k], short_get.at[sweep, group, k], peer,
            )
            for k, peer in enumerate(peers)
        ]

    low_lane = lax.broadcasted_iota(jnp.int32, (1, C), 1) < HALF

    def one_hot(cells):
        return (lax.broadcasted_iota(jnp.int32, (C, C), 0) == cells).astype(F32).astype(BF16)

    def tables(kind, cols, first):
        place = cols - first
        own = jnp.where(low_lane, place[1:2], place[0:1])
        reach = jnp.where(low_lane, place[0:1], place[1:2])
        hot_near[kind] = one_hot(own)
        left = jnp.where(reach < 0, reach + HALF, -1)
        right = jnp.where(reach >= C, reach - HALF, -1)
        rim = jnp.maximum(left, right)
        swapped = jnp.where(rim < 0, rim, lax.rem(rim + HALF, C))
        hot_far[kind, 0] = one_hot(rim)
        hot_far[kind, 1] = one_hot(swapped)
        hot_far[kind, 2] = one_hot(reach)

    field[...] = jnp.zeros_like(field)

    def widen_diag(kind, start, stop):
        sub = lax.broadcasted_iota(jnp.int32, (8, C), 0)

        def step(block, carry):
            low = pl.multiple_of(block * 8, 8)
            total = jnp.zeros((8, C), F32)
            for i in range(8):
                diag[kind, low + i] = diag_in[kind, low + i].astype(F32)
                total = jnp.where(sub == i, diag[kind, low + i, pl.ds(low, 8), :], total)
            scale[kind, pl.ds(low, 8), :] = 1.0 / total
            return carry

        lax.fori_loop(start // 8, stop // 8, step, 0)

    def widen_off(target, first, start, stop):
        mask = lane_low(S)

        def step(block, carry):
            for i in range(4):
                row = start + block * 4 + i
                target[row] = jnp.where(mask, off_in[row, first], off_in[row, 1 - first]).astype(F32)
            return carry

        lax.fori_loop(0, (stop - start) // 4, step, 0)

    def smooth(kind, group):
        for r in range(PAIR):
            u[r] = q[group, r] * scale[kind]

        def step(block, carry):
            base = block * 8
            sums = products(
                [
                    (
                        lambda i, low: diag[kind, base + i, low : low + 8, :],
                        lambda r, low: u[r, low : low + 8, :],
                    )
                ]
            )
            rows = pl.ds(pl.multiple_of(base, 8), 8)
            for r in range(PAIR):
                total = fold_rows([sums[i][r] for i in range(8)])
                change = (OMEGA * scale[kind, rows, :]) * (2.0 * q[group, r, rows, :] - total)
                field[kind, group, r, rows, :] = field[kind, group, r, rows, :] + change
            return carry

        lax.fori_loop(0, S // 8, step, 0)

    def start_rims(rim, group, kind):
        rounded = field[kind, group].astype(BF16)
        xb[group] = rounded
        xw[group] = rounded.astype(F32)
        lower = pltpu.roll(field[kind, group, : PAIR // 2].reshape(SPAN, C), HALF, 1)
        upper = field[kind, group, PAIR // 2 :].reshape(SPAN, C)
        mask = lane_low(SPAN)
        send_rim[rim, group, 0] = jnp.where(mask, lower, upper).astype(BF16)
        send_rim[rim, group, 1] = jnp.where(mask, upper, lower).astype(BF16)
        for copy in rim_copies(rim, group, kind):
            copy.start()

    def place(kind):
        return (0, 0, S) if kind == FINE else (level * ROWS, S, ROWS)

    def apply_near(group, kind):
        near[...] = jnp.dot(
            xb[group].reshape(PAIR * S, C), hot_near[kind], preferred_element_type=F32
        ).reshape(PAIR, S, C)
        start, first, rows = place(kind)

        def step(block, carry):
            base = block * 8
            sums = products(
                [
                    (
                        lambda i, low: diag[kind, start + base + i, low : low + 8, :],
                        lambda r, low: xw[group, r, low : low + 8, :],
                    ),
                    (
                        lambda i, low: off_near[first + base + i, low : low + 8, :],
                        lambda r, low: near[r, low : low + 8, :],
                    ),
                ]
            )
            for i in range(8):
                for r in range(PAIR):
                    acc[group, block, i * PAIR + r] = sums[i][r]
            return carry

        lax.fori_loop(0, rows // 8, step, 0)

    def finish_rims(rim, group, kind):
        for copy in rim_copies(rim, group, kind):
            copy.wait_recv()
        left = get_rim[rim, group, 0]
        right = get_rim[rim, group, 1]
        mask = lane_low(SPAN)
        for k in range(2):
            own = slice(k * PAIR // 2, (k + 1) * PAIR // 2)
            ends = jnp.where(mask, left, right) if k == 0 else jnp.where(mask, right, left)
            value = jnp.dot(ends, hot_far[kind, k], preferred_element_type=F32)
            value = value + jnp.dot(
                xb[group, own].reshape(SPAN, C), hot_far[kind, 2], preferred_element_type=F32
            )
            far[own] = value.reshape(PAIR // 2, S, C)
        start, first, count = place(kind)

        def step(block, carry):
            base = block * 8
            held = [[acc[group, block, i * PAIR + r] for r in range(PAIR)] for i in range(8)]
            sums = products(
                [
                    (
                        lambda i, low: off_far[first + base + i, low : low + 8, :],
                        lambda r, low: far[r, low : low + 8, :],
                    )
                ],
                held,
            )
            rows = pl.ds(pl.multiple_of(start + base, 8), 8)
            for r in range(PAIR):
                total = fold_rows([sums[i][r] for i in range(8)])
                q[group, r, rows, :] = fixed[kind, group, r, rows, :] - total
            return carry

        lax.fori_loop(0, count // 8, step, 0)

    def split_dot(value, dims):
        high = value.astype(BF16)
        low = (value - high.astype(F32)).astype(BF16)
        return sum(
            lax.dot_general(part, member[...], (dims, ((), ())), preferred_element_type=F32)
            for part in (high, low)
        )

    own_rows = pl.ds(pl.multiple_of(level * ROWS, ROWS), ROWS)

    def send_residual(group):
        part = split_dot(q[group].reshape(PAIR * S, C), ((1,), (1,)))
        send_part[group] = part.astype(BF16)
        for copy in part_copies(group):
            copy.start()

    def sum_residual(group):
        for copy in part_copies(group):
            copy.wait_recv()
        total = send_part[group].astype(F32)
        for k in range(levels - 1):
            total = total + get_part[group, k].astype(F32)
        fixed[COARSE, group] = total.reshape(PAIR, S, C)
        q[group] = total.reshape(PAIR, S, C)

    def send_shortfall(sweep, group):
        for r in range(PAIR):
            value = q[group, r, own_rows, :].astype(BF16)
            send_short[sweep, group, r] = value
            q[group, r, own_rows, :] = value.astype(F32)
        for copy in short_copies(sweep, group):
            copy.start()

    def join_shortfall(sweep, group):
        for k, copy in enumerate(short_copies(sweep, group)):
            copy.wait_recv()
            source = lax.rem(level + levels - (k + 1), levels)
            rows = pl.ds(pl.multiple_of(source * ROWS, ROWS), ROWS)
            for r in range(PAIR):
                q[group, r, rows, :] = get_short[sweep, group, k, r].astype(F32)

    groups = range(GROUPS)

    def save(group):
        own = slice(group * PAIR, (group + 1) * PAIR)
        return pltpu.make_async_copy(field.at[FINE, group], out_hbm.at[own], save_sem.at[group])

    for k in range(2):
        load_diag[k].wait()
        widen_diag(FINE, k * half, (k + 1) * half)
    load_rhs.wait()
    for r in range(R):
        value = rhs_in[:, r, :]
        fixed[FINE, r // PAIR, r % PAIR] = value
        q[r // PAIR, r % PAIR] = value
    for group in groups:
        smooth(FINE, group)
        if group == 0:
            pl.semaphore_wait(barrier, len(partners))
        start_rims(0, group, FINE)
    load_cols.wait()
    tables(FINE, cols_ref[...], index * C)
    for k in range(2):
        load_off[k].wait()
        widen_off(off_near, 1, k * half, (k + 1) * half)
    for group in groups:
        apply_near(group, FINE)
    widen_off(off_far, 0, 0, S)
    for copy in load_coarse:
        copy.wait()
    member[...] = one_hot(agg_ref[...] - space * C)
    for group in groups:
        finish_rims(0, group, FINE)
        smooth(FINE, group)
        start_rims(1, group, FINE)
        apply_near(group, FINE)
    for group in groups:
        finish_rims(1, group, FINE)
        send_residual(group)
    tables(COARSE, ccols_ref[...], space * C)
    widen_diag(COARSE, 0, S)
    widen_off(off_near, 1, S, S + ROWS)
    widen_off(off_far, 0, S, S + ROWS)
    for group in groups:
        sum_residual(group)
        smooth(COARSE, group)
        start_rims(2, group, COARSE)
        apply_near(group, COARSE)
    for sweep in range(2):
        for group in groups:
            finish_rims(2 + sweep, group, COARSE)
            send_shortfall(sweep, group)
        for group in groups:
            join_shortfall(sweep, group)
            smooth(COARSE, group)
            if sweep == 0:
                start_rims(3, group, COARSE)
                apply_near(group, COARSE)
            else:
                spread = split_dot(field[COARSE, group].reshape(PAIR * S, C), ((1,), (0,)))
                field[FINE, group] = field[FINE, group] + spread.reshape(PAIR, S, C)
                start_rims(4, group, FINE)
                apply_near(group, FINE)
    for group in groups:
        finish_rims(4, group, FINE)
        smooth(FINE, group)
        save(group).start()
    for group in groups:
        save(group).wait()
        for rim in range(RIMS):
            for copy in rim_copies(rim, group, FINE):
                copy.wait_send()
        for copy in part_copies(group):
            copy.wait_send()
        for sweep in range(2):
            for copy in short_copies(sweep, group):
                copy.wait_send()


def local(sizes, rhs, fine_diag, fine_off, fine_cols, aggregates, coarse_diag, coarse_off, coarse_cols):
    others = sizes[1] - 1
    hbm = pl.BlockSpec(memory_space=pl.ANY)
    dma = pltpu.SemaphoreType.DMA
    result = pl.pallas_call(
        functools.partial(kernel, sizes),
        out_shape=jax.ShapeDtypeStruct((R, S, C), F32),
        in_specs=[hbm] * 8,
        out_specs=hbm,
        scratch_shapes=[
            pltpu.VMEM((2, C), jnp.int32),
            pltpu.VMEM((1, C), jnp.int32),
            pltpu.VMEM((2, C), jnp.int32),
            pltpu.VMEM((S, R, C), F32),
            pltpu.VMEM((2, S, S, C), BF16),
            pltpu.VMEM((S + ROWS, 2, S, C), BF16),
            pltpu.VMEM((2, S, S, C), F32),
            pltpu.VMEM((S + ROWS, S, C), F32),
            pltpu.VMEM((S + ROWS, S, C), F32),
            pltpu.VMEM((2, S, C), F32),
            pltpu.VMEM((2, GROUPS, PAIR, S, C), F32),
            pltpu.VMEM((2, GROUPS, PAIR, S, C), F32),
            pltpu.VMEM((GROUPS, PAIR, S, C), F32),
            pltpu.VMEM((PAIR, S, C), F32),
            pltpu.VMEM((GROUPS, PAIR, S, C), BF16),
            pltpu.VMEM((GROUPS, PAIR, S, C), F32),
            pltpu.VMEM((PAIR, S, C), F32),
            pltpu.VMEM((PAIR, S, C), F32),
            pltpu.VMEM((GROUPS, S // 8, 8 * PAIR, 8, C), F32),
            pltpu.VMEM((2, C, C), BF16),
            pltpu.VMEM((2, 3, C, C), BF16),
            pltpu.VMEM((C, C), BF16),
            pltpu.VMEM((RIMS, GROUPS, 2, SPAN, C), BF16),
            pltpu.VMEM((RIMS, GROUPS, 2, SPAN, C), BF16),
            pltpu.VMEM((GROUPS, PAIR * S, C), BF16),
            pltpu.VMEM((GROUPS, others, PAIR * S, C), BF16),
            pltpu.VMEM((2, GROUPS, PAIR, ROWS, C), BF16),
            pltpu.VMEM((2, GROUPS, others, PAIR, ROWS, C), BF16),
            dma((10,)),
            dma((GROUPS,)),
            dma((RIMS, GROUPS, 2)),
            dma((RIMS, GROUPS, 2)),
            dma((GROUPS, others)),
            dma((GROUPS, others)),
            dma((2, GROUPS, others)),
            dma((2, GROUPS, others)),
        ],
        compiler_params=pltpu.CompilerParams(
            collective_id=0, has_side_effects=True, vmem_limit_bytes=63 * 1024 * 1024
        ),
        name="vcycle",
    )(
        rhs, fine_diag, fine_off, fine_cols, aggregates.reshape(1, C),
        coarse_diag, coarse_off, coarse_cols,
    )
    return result.transpose(1, 0, 2)


def solution(mesh):
    placed = (
        P(None, None, ("space", "level")),
        P(None, None, ("space", "level")),
        P(None, None, None, ("space", "level")),
        P(None, ("space", "level")),
        P(("space", "level")),
        P(None, None, "space"),
        P("level", None, None, "space"),
        P(None, "space"),
    )
    sizes = (mesh.shape["space"], mesh.shape["level"])
    return jax.shard_map(
        functools.partial(local, sizes),
        mesh=mesh,
        in_specs=placed,
        out_specs=P(None, None, ("space", "level")),
        check_vma=False,
    )
```

```python
import functools

import jax
import jax.numpy as jnp
from jax import lax
from jax.experimental import pallas as pl
from jax.experimental.pallas import tpu as pltpu
from jax.sharding import PartitionSpec as P

OMEGA = 0.7
S = 64
R = 4
GROUPS = 2
PAIR = R // GROUPS
C = 128
HALF = 64
ROWS = 16
SPAN = PAIR // 2 * S
FINE, COARSE = 0, 1
RIM_KINDS = (FINE, FINE, COARSE, COARSE, FINE)
MESH = pl.DeviceIdType.MESH
F32 = jnp.float32
BF16 = jnp.bfloat16


def lane_low(rows):
    return lax.broadcasted_iota(jnp.int32, (rows, C), 1) < HALF


def fold_rows(parts):
    sub = lax.broadcasted_iota(jnp.int32, (8, C), 0)
    four = sub < 4
    two = lax.rem(sub, 4) < 2
    one = lax.rem(sub, 2) < 1
    level = [
        jnp.where(four, parts[i], parts[i + 4])
        + pltpu.roll(jnp.where(four, parts[i + 4], parts[i]), 4, 0)
        for i in range(4)
    ]
    level = [
        jnp.where(
            two,
            level[i] + pltpu.roll(level[i], 6, 0),
            level[i + 2] + pltpu.roll(level[i + 2], 2, 0),
        )
        for i in range(2)
    ]
    return jnp.where(
        one,
        level[0] + pltpu.roll(level[0], 7, 0),
        level[1] + pltpu.roll(level[1], 1, 0),
    )


def products(terms, start=None):
    sums = [[None] * PAIR for _ in range(8)] if start is None else start
    for load, vector in terms:
        for low in range(0, S, 8):
            pieces = [vector(r, low) for r in range(PAIR)]
            for i in range(8):
                matrix = load(i, low)
                for r in range(PAIR):
                    piece = matrix * pieces[r]
                    sums[i][r] = piece if sums[i][r] is None else sums[i][r] + piece
    return sums


def kernel(
    sizes,
    rhs_hbm, diag_hbm, off_hbm, cols_hbm, agg_hbm, cdiag_hbm, coff_hbm, ccols_hbm,
    out_hbm,
    cols_ref, agg_ref, ccols_ref, rhs_in, diag_in, off_in, diag, off_near, off_far, scale, fixed, field, q, u, xb, xw, near, far, acc,
    hot_near, hot_far, member,
    send_rim, get_rim, send_part, get_part, send_short, get_short,
    load_sem, save_sem, rim_send, rim_get, part_send, part_get, short_send, short_get,
):
    spaces, levels = sizes
    space = lax.axis_index("space")
    level = lax.axis_index("level")
    index = space * levels + level
    count = spaces * levels
    after = lax.rem(index + 1, count)
    before = lax.rem(index + count - 1, count)
    fine_next = (lax.div(after, levels), lax.rem(after, levels))
    fine_last = (lax.div(before, levels), lax.rem(before, levels))
    space_next = (lax.rem(space + 1, spaces), level)
    space_last = (lax.rem(space + spaces - 1, spaces), level)
    peers = [(space, lax.rem(level + k, levels)) for k in range(1, levels)]

    beyond = {
        FINE: (index < count - 1, index > 0),
        COARSE: (space < spaces - 1, space > 0),
    }
    targets = {FINE: (fine_next, fine_last), COARSE: (space_next, space_last)}

    barrier = pltpu.get_barrier_semaphore()
    awaited = levels - 1

    def greet(partner):
        pl.semaphore_signal(barrier, inc=1, device_id=partner, device_id_type=MESH)

    for partner in peers:
        greet(partner)
    for kind in (FINE, COARSE):
        for k in range(2):
            awaited = awaited + beyond[kind][k].astype(jnp.int32)
            pl.when(beyond[kind][k])(functools.partial(greet, targets[kind][k]))

    def load(k, source, target):
        return pltpu.make_async_copy(source, target, load_sem.at[k])

    half = S // 2
    load_diag = [
        load(k, diag_hbm.at[k * half : (k + 1) * half], diag_in.at[FINE, k * half : (k + 1) * half])
        for k in range(2)
    ]
    load_rhs = load(2, rhs_hbm, rhs_in)
    load_cols = load(3, cols_hbm, cols_ref)
    load_off = [
        load(4 + k, off_hbm.at[k * half : (k + 1) * half], off_in.at[k * half : (k + 1) * half])
        for k in range(2)
    ]
    load_coarse = [
        load(6, agg_hbm, agg_ref),
        load(7, ccols_hbm, ccols_ref),
        load(8, cdiag_hbm, diag_in.at[COARSE]),
        load(9, coff_hbm, off_in.at[S : S + ROWS]),
    ]
    for copy in load_diag + [load_rhs, load_cols] + load_off + load_coarse:
        copy.start()

    def remote(source, target, sent, got, device):
        return pltpu.make_async_remote_copy(
            src_ref=source, dst_ref=target, send_sem=sent, recv_sem=got,
            device_id=device, device_id_type=MESH,
        )

    def rim_copies(rim, group, kind):
        return [
            remote(
                send_rim.at[rim, group, k], get_rim.at[rim, group, k],
                rim_send.at[rim, group, k], rim_get.at[rim, group, k], targets[kind][k],
            )
            for k in range(2)
        ]

    def part_copies(group):
        return [
            remote(
                send_part.at[group], get_part.at[group, k],
                part_send.at[group, k], part_get.at[group, k], peer,
            )
            for k, peer in enumerate(peers)
        ]

    def short_copies(sweep, group):
        return [
            remote(
                send_short.at[sweep, group], get_short.at[sweep, group, k],
                short_send.at[sweep, group, k], short_get.at[sweep, group, k], peer,
            )
            for k, peer in enumerate(peers)
        ]

    low_lane = lax.broadcasted_iota(jnp.int32, (1, C), 1) < HALF

    def one_hot(cells):
        return (lax.broadcasted_iota(jnp.int32, (C, C), 0) == cells).astype(F32).astype(BF16)

    def tables(kind, cols, first):
        place = cols - first
        own = jnp.where(low_lane, place[1:2], place[0:1])
        reach = jnp.where(low_lane, place[0:1], place[1:2])
        hot_near[kind] = one_hot(own)
        left = jnp.where(reach < 0, reach + HALF, -1)
        right = jnp.where(reach >= C, reach - HALF, -1)
        rim = jnp.maximum(left, right)
        swapped = jnp.where(rim < 0, rim, lax.rem(rim + HALF, C))
        hot_far[kind, 0] = one_hot(rim)
        hot_far[kind, 1] = one_hot(swapped)
        hot_far[kind, 2] = one_hot(reach)

    field[...] = jnp.zeros_like(field)

    def clear(kind, k):
        for rim in range(len(RIM_KINDS)):
            if RIM_KINDS[rim] == kind:
                get_rim[rim, :, k] = jnp.zeros((GROUPS, SPAN, C), BF16)

    for kind in (FINE, COARSE):
        for k in range(2):
            pl.when(~beyond[kind][1 - k])(functools.partial(clear, kind, k))

    def widen_diag(kind, start, stop):
        sub = lax.broadcasted_iota(jnp.int32, (8, C), 0)

        def step(block, carry):
            low = pl.multiple_of(block * 8, 8)
            total = jnp.zeros((8, C), F32)
            for i in range(8):
                diag[kind, low + i] = diag_in[kind, low + i].astype(F32)
                total = jnp.where(sub == i, diag[kind, low + i, pl.ds(low, 8), :], total)
            scale[kind, pl.ds(low, 8), :] = 1.0 / total
            return carry

        lax.fori_loop(start // 8, stop // 8, step, 0)

    def widen_off(target, first, start, stop):
        mask = lane_low(S)

        def step(block, carry):
            for i in range(4):
                row = start + block * 4 + i
                target[row] = jnp.where(mask, off_in[row, first], off_in[row, 1 - first]).astype(F32)
            return carry

        lax.fori_loop(0, (stop - start) // 4, step, 0)

    def smooth(kind, group):
        for r in range(PAIR):
            u[r] = q[group, r] * scale[kind]

        def step(block, carry):
            base = block * 8
            sums = products(
                [
                    (
                        lambda i, low: diag[kind, base + i, low : low + 8, :],
                        lambda r, low: u[r, low : low + 8, :],
                    )
                ]
            )
            rows = pl.ds(pl.multiple_of(base, 8), 8)
            for r in range(PAIR):
                total = fold_rows([sums[i][r] for i in range(8)])
                change = (OMEGA * scale[kind, rows, :]) * (2.0 * q[group, r, rows, :] - total)
                field[kind, group, r, rows, :] = field[kind, group, r, rows, :] + change
            return carry

        lax.fori_loop(0, S // 8, step, 0)

    def start_rims(rim, group, kind):
        rounded = field[kind, group].astype(BF16)
        xb[group] = rounded
        xw[group] = rounded.astype(F32)
        lower = pltpu.roll(field[kind, group, : PAIR // 2].reshape(SPAN, C), HALF, 1)
        upper = field[kind, group, PAIR // 2 :].reshape(SPAN, C)
        mask = lane_low(SPAN)
        send_rim[rim, group, 0] = jnp.where(mask, lower, upper).astype(BF16)
        send_rim[rim, group, 1] = jnp.where(mask, upper, lower).astype(BF16)
        for k, copy in enumerate(rim_copies(rim, group, kind)):
            pl.when(beyond[kind][k])(copy.start)

    def place(kind):
        return (0, 0, S) if kind == FINE else (level * ROWS, S, ROWS)

    def apply_near(group, kind):
        near[...] = jnp.dot(
            xb[group].reshape(PAIR * S, C), hot_near[kind], preferred_element_type=F32
        ).reshape(PAIR, S, C)
        start, first, rows = place(kind)

        def step(block, carry):
            base = block * 8
            sums = products(
                [
                    (
                        lambda i, low: diag[kind, start + base + i, low : low + 8, :],
                        lambda r, low: xw[group, r, low : low + 8, :],
                    ),
                    (
                        lambda i, low: off_near[first + base + i, low : low + 8, :],
                        lambda r, low: near[r, low : low + 8, :],
                    ),
                ]
            )
            for i in range(8):
                for r in range(PAIR):
                    acc[group, block, i * PAIR + r] = sums[i][r]
            return carry

        lax.fori_loop(0, rows // 8, step, 0)

    def finish_rims(rim, group, kind):
        for k, copy in enumerate(rim_copies(rim, group, kind)):
            pl.when(beyond[kind][1 - k])(copy.wait_recv)
        left = get_rim[rim, group, 0]
        right = get_rim[rim, group, 1]
        mask = lane_low(SPAN)
        for k in range(2):
            own = slice(k * PAIR // 2, (k + 1) * PAIR // 2)
            ends = jnp.where(mask, left, right) if k == 0 else jnp.where(mask, right, left)
            value = jnp.dot(ends, hot_far[kind, k], preferred_element_type=F32)
            value = value + jnp.dot(
                xb[group, own].reshape(SPAN, C), hot_far[kind, 2], preferred_element_type=F32
            )
            far[own] = value.reshape(PAIR // 2, S, C)
        start, first, count = place(kind)

        def step(block, carry):
            base = block * 8
            held = [[acc[group, block, i * PAIR + r] for r in range(PAIR)] for i in range(8)]
            sums = products(
                [
                    (
                        lambda i, low: off_far[first + base + i, low : low + 8, :],
                        lambda r, low: far[r, low : low + 8, :],
                    )
                ],
                held,
            )
            rows = pl.ds(pl.multiple_of(start + base, 8), 8)
            for r in range(PAIR):
                total = fold_rows([sums[i][r] for i in range(8)])
                q[group, r, rows, :] = fixed[kind, group, r, rows, :] - total
            return carry

        lax.fori_loop(0, count // 8, step, 0)

    def split_dot(value, dims):
        high = value.astype(BF16)
        low = (value - high.astype(F32)).astype(BF16)
        return sum(
            lax.dot_general(part, member[...], (dims, ((), ())), preferred_element_type=F32)
            for part in (high, low)
        )

    own_rows = pl.ds(pl.multiple_of(level * ROWS, ROWS), ROWS)

    def send_residual(group):
        part = split_dot(q[group].reshape(PAIR * S, C), ((1,), (1,)))
        send_part[group] = part.astype(BF16)
        for copy in part_copies(group):
            copy.start()

    def sum_residual(group):
        for copy in part_copies(group):
            copy.wait_recv()
        total = send_part[group].astype(F32)
        for k in range(levels - 1):
            total = total + get_part[group, k].astype(F32)
        fixed[COARSE, group] = total.reshape(PAIR, S, C)
        q[group] = total.reshape(PAIR, S, C)

    def send_shortfall(sweep, group):
        for r in range(PAIR):
            value = q[group, r, own_rows, :].astype(BF16)
            send_short[sweep, group, r] = value
            q[group, r, own_rows, :] = value.astype(F32)
        for copy in short_copies(sweep, group):
            copy.start()

    def join_shortfall(sweep, group):
        for k, copy in enumerate(short_copies(sweep, group)):
            copy.wait_recv()
            source = lax.rem(level + levels - (k + 1), levels)
            rows = pl.ds(pl.multiple_of(source * ROWS, ROWS), ROWS)
            for r in range(PAIR):
                q[group, r, rows, :] = get_short[sweep, group, k, r].astype(F32)

    groups = range(GROUPS)

    def save(group):
        own = slice(group * PAIR, (group + 1) * PAIR)
        return pltpu.make_async_copy(field.at[FINE, group], out_hbm.at[own], save_sem.at[group])

    for k in range(2):
        load_diag[k].wait()
        widen_diag(FINE, k * half, (k + 1) * half)
    load_rhs.wait()
    for r in range(R):
        value = rhs_in[:, r, :]
        fixed[FINE, r // PAIR, r % PAIR] = value
        q[r // PAIR, r % PAIR] = value
    for group in groups:
        smooth(FINE, group)
        if group == 0:
            pl.semaphore_wait(barrier, awaited)
        start_rims(0, group, FINE)
    load_cols.wait()
    tables(FINE, cols_ref[...], index * C)
    for k in range(2):
        load_off[k].wait()
        widen_off(off_near, 1, k * half, (k + 1) * half)
    for group in groups:
        apply_near(group, FINE)
    widen_off(off_far, 0, 0, S)
    for copy in load_coarse:
        copy.wait()
    member[...] = one_hot(agg_ref[...] - space * C)
    for group in groups:
        finish_rims(0, group, FINE)
        smooth(FINE, group)
        start_rims(1, group, FINE)
        apply_near(group, FINE)
    for group in groups:
        finish_rims(1, group, FINE)
        send_residual(group)
    tables(COARSE, ccols_ref[...], space * C)
    widen_diag(COARSE, 0, S)
    widen_off(off_near, 1, S, S + ROWS)
    widen_off(off_far, 0, S, S + ROWS)
    for group in groups:
        sum_residual(group)
        smooth(COARSE, group)
        start_rims(2, group, COARSE)
        apply_near(group, COARSE)
    for sweep in range(2):
        for group in groups:
            finish_rims(2 + sweep, group, COARSE)
            send_shortfall(sweep, group)
        for group in groups:
            join_shortfall(sweep, group)
            smooth(COARSE, group)
            if sweep == 0:
                start_rims(3, group, COARSE)
                apply_near(group, COARSE)
            else:
                spread = split_dot(field[COARSE, group].reshape(PAIR * S, C), ((1,), (0,)))
                field[FINE, group] = field[FINE, group] + spread.reshape(PAIR, S, C)
                start_rims(4, group, FINE)
                apply_near(group, FINE)
    for group in groups:
        finish_rims(4, group, FINE)
        smooth(FINE, group)
        save(group).start()
    for group in groups:
        save(group).wait()
        for rim in range(len(RIM_KINDS)):
            kind = RIM_KINDS[rim]
            for k, copy in enumerate(rim_copies(rim, group, kind)):
                pl.when(beyond[kind][k])(copy.wait_send)
        for copy in part_copies(group):
            copy.wait_send()
        for sweep in range(2):
            for copy in short_copies(sweep, group):
                copy.wait_send()


def local(sizes, rhs, fine_diag, fine_off, fine_cols, aggregates, coarse_diag, coarse_off, coarse_cols):
    others = sizes[1] - 1
    hbm = pl.BlockSpec(memory_space=pl.ANY)
    dma = pltpu.SemaphoreType.DMA
    result = pl.pallas_call(
        functools.partial(kernel, sizes),
        out_shape=jax.ShapeDtypeStruct((R, S, C), F32),
        in_specs=[hbm] * 8,
        out_specs=hbm,
        scratch_shapes=[
            pltpu.VMEM((2, C), jnp.int32),
            pltpu.VMEM((1, C), jnp.int32),
            pltpu.VMEM((2, C), jnp.int32),
            pltpu.VMEM((S, R, C), F32),
            pltpu.VMEM((2, S, S, C), BF16),
            pltpu.VMEM((S + ROWS, 2, S, C), BF16),
            pltpu.VMEM((2, S, S, C), F32),
            pltpu.VMEM((S + ROWS, S, C), F32),
            pltpu.VMEM((S + ROWS, S, C), F32),
            pltpu.VMEM((2, S, C), F32),
            pltpu.VMEM((2, GROUPS, PAIR, S, C), F32),
            pltpu.VMEM((2, GROUPS, PAIR, S, C), F32),
            pltpu.VMEM((GROUPS, PAIR, S, C), F32),
            pltpu.VMEM((PAIR, S, C), F32),
            pltpu.VMEM((GROUPS, PAIR, S, C), BF16),
            pltpu.VMEM((GROUPS, PAIR, S, C), F32),
            pltpu.VMEM((PAIR, S, C), F32),
            pltpu.VMEM((PAIR, S, C), F32),
            pltpu.VMEM((GROUPS, S // 8, 8 * PAIR, 8, C), F32),
            pltpu.VMEM((2, C, C), BF16),
            pltpu.VMEM((2, 3, C, C), BF16),
            pltpu.VMEM((C, C), BF16),
            pltpu.VMEM((len(RIM_KINDS), GROUPS, 2, SPAN, C), BF16),
            pltpu.VMEM((len(RIM_KINDS), GROUPS, 2, SPAN, C), BF16),
            pltpu.VMEM((GROUPS, PAIR * S, C), BF16),
            pltpu.VMEM((GROUPS, others, PAIR * S, C), BF16),
            pltpu.VMEM((2, GROUPS, PAIR, ROWS, C), BF16),
            pltpu.VMEM((2, GROUPS, others, PAIR, ROWS, C), BF16),
            dma((10,)),
            dma((GROUPS,)),
            dma((len(RIM_KINDS), GROUPS, 2)),
            dma((len(RIM_KINDS), GROUPS, 2)),
            dma((GROUPS, others)),
            dma((GROUPS, others)),
            dma((2, GROUPS, others)),
            dma((2, GROUPS, others)),
        ],
        compiler_params=pltpu.CompilerParams(
            collective_id=0, has_side_effects=True, vmem_limit_bytes=63 * 1024 * 1024
        ),
        name="vcycle",
    )(
        rhs, fine_diag, fine_off, fine_cols, aggregates.reshape(1, C),
        coarse_diag, coarse_off, coarse_cols,
    )
    return result.transpose(1, 0, 2)


def solution(mesh):
    placed = (
        P(None, None, ("space", "level")),
        P(None, None, ("space", "level")),
        P(None, None, None, ("space", "level")),
        P(None, ("space", "level")),
        P(("space", "level")),
        P(None, None, "space"),
        P("level", None, None, "space"),
        P(None, "space"),
    )
    sizes = (mesh.shape["space"], mesh.shape["level"])
    return jax.shard_map(
        functools.partial(local, sizes),
        mesh=mesh,
        in_specs=placed,
        out_specs=P(None, None, ("space", "level")),
        check_vma=False,
    )
```

```python
import functools

import jax
import jax.numpy as jnp
from jax import lax
from jax.experimental import pallas as pl
from jax.experimental.pallas import tpu as pltpu
from jax.sharding import PartitionSpec as P

OMEGA = 0.7
S = 64
R = 4
GROUPS = 2
PAIR = R // GROUPS
C = 128
HALF = 64
ROWS = 16
PIECE = 4
SPAN = PAIR * S // 2
FINE, COARSE = 0, 1
RIM_KINDS = (FINE, FINE, COARSE, COARSE, FINE)
MESH = pl.DeviceIdType.MESH
F32 = jnp.float32
BF16 = jnp.bfloat16


def lane_low(rows):
    return lax.broadcasted_iota(jnp.int32, (rows, C), 1) < HALF


def fold_rows(parts):
    sub = lax.broadcasted_iota(jnp.int32, (8, C), 0)
    four = sub < 4
    two = lax.rem(sub, 4) < 2
    one = lax.rem(sub, 2) < 1
    level = [
        jnp.where(four, parts[i], parts[i + 4])
        + pltpu.roll(jnp.where(four, parts[i + 4], parts[i]), 4, 0)
        for i in range(4)
    ]
    level = [
        jnp.where(
            two,
            level[i] + pltpu.roll(level[i], 6, 0),
            level[i + 2] + pltpu.roll(level[i + 2], 2, 0),
        )
        for i in range(2)
    ]
    return jnp.where(
        one,
        level[0] + pltpu.roll(level[0], 7, 0),
        level[1] + pltpu.roll(level[1], 1, 0),
    )


def products(terms, start=None):
    sums = [[None] * PAIR for _ in range(8)] if start is None else start
    for load, vector in terms:
        for low in range(0, S, 8):
            pieces = [vector(r, low) for r in range(PAIR)]
            for i in range(8):
                matrix = load(i, low)
                for r in range(PAIR):
                    piece = matrix * pieces[r]
                    sums[i][r] = piece if sums[i][r] is None else sums[i][r] + piece
    return sums


def kernel(
    sizes,
    rhs_hbm, diag_hbm, off_hbm, cols_hbm, agg_hbm, cdiag_hbm, coff_hbm, ccols_hbm,
    out_hbm,
    cols_ref, agg_ref, ccols_ref, rhs_in, diag_in, off_in, diag, off_near, off_far, scale, fixed, field, q, u, xb, xw, near, far, acc,
    hot_near, hot_far, member,
    send_rim, get_rim, send_part, get_part, send_short, get_short, send_far, get_far,
    load_sem, save_sem, rim_send, rim_get, part_send, part_get, short_send, short_get, far_send, far_get,
):
    spaces, levels = sizes
    space = lax.axis_index("space")
    level = lax.axis_index("level")
    index = space * levels + level
    count = spaces * levels
    after = lax.rem(index + 1, count)
    before = lax.rem(index + count - 1, count)
    fine_next = (lax.div(after, levels), lax.rem(after, levels))
    fine_last = (lax.div(before, levels), lax.rem(before, levels))
    space_next = (lax.rem(space + 1, spaces), level)
    space_last = (lax.rem(space + spaces - 1, spaces), level)
    peers = [(space, lax.rem(level + k, levels)) for k in range(1, levels)]

    beyond = {
        FINE: (index < count - 1, index > 0),
        COARSE: (space < spaces - 1, space > 0),
    }
    targets = {FINE: (fine_next, fine_last), COARSE: (space_next, space_last)}

    far_first = sorted(range(levels - 1), key=lambda k: -min(k + 1, levels - 1 - k))

    barrier = pltpu.get_barrier_semaphore()
    awaited = levels - 1

    def greet(partner):
        pl.semaphore_signal(barrier, inc=1, device_id=partner, device_id_type=MESH)

    for partner in peers:
        greet(partner)
    for kind in (FINE, COARSE):
        for k in range(2):
            awaited = awaited + beyond[kind][k].astype(jnp.int32)
            pl.when(beyond[kind][k])(functools.partial(greet, targets[kind][k]))

    def load(k, source, target):
        return pltpu.make_async_copy(source, target, load_sem.at[k])

    half = S // 2
    load_diag = [
        load(k, diag_hbm.at[k * half : (k + 1) * half], diag_in.at[FINE, k * half : (k + 1) * half])
        for k in range(2)
    ]
    load_rhs = load(2, rhs_hbm, rhs_in)
    load_cols = load(3, cols_hbm, cols_ref)
    load_off = [
        load(4 + k, off_hbm.at[k * half : (k + 1) * half], off_in.at[k * half : (k + 1) * half])
        for k in range(2)
    ]
    load_coff = load(9, coff_hbm, off_in.at[S : S + ROWS])
    load_coarse = [
        load(6, agg_hbm, agg_ref),
        load(7, ccols_hbm, ccols_ref),
        load(8, cdiag_hbm, diag_in.at[COARSE]),
    ]
    for copy in load_diag + [load_rhs, load_coff, load_cols] + load_off + load_coarse:
        copy.start()

    def remote(source, target, sent, got, device):
        return pltpu.make_async_remote_copy(
            src_ref=source, dst_ref=target, send_sem=sent, recv_sem=got,
            device_id=device, device_id_type=MESH,
        )

    def rim_copies(rim, group, kind):
        return [
            remote(
                send_rim.at[rim, group, k], get_rim.at[rim, group, k],
                rim_send.at[rim, group, k], rim_get.at[rim, group, k], targets[kind][k],
            )
            for k in range(2)
        ]

    def part_copies(group):
        return [
            remote(
                send_part.at[group], get_part.at[group, k],
                part_send.at[group, k], part_get.at[group, k], peer,
            )
            for k, peer in enumerate(peers)
        ]

    def short_copies(sweep, group):
        return [
            remote(
                send_short.at[sweep, group], get_short.at[sweep, group, k],
                short_send.at[sweep, group, k], short_get.at[sweep, group, k], peer,
            )
            for k, peer in enumerate(peers)
        ]

    def far_copies(piece):
        rows = slice(piece * PIECE, (piece + 1) * PIECE)
        return [
            remote(
                send_far.at[rows], get_far.at[k, rows],
                far_send.at[piece, k], far_get.at[piece, k], peer,
            )
            for k, peer in enumerate(peers)
        ]

    def start_far(piece):
        for k in far_first:
            far_copies(piece)[k].start()

    def source_rows(k, first=0):
        source = lax.rem(level + levels - (k + 1), levels)
        return first + pl.multiple_of(source * ROWS, ROWS)

    low_lane = lax.broadcasted_iota(jnp.int32, (1, C), 1) < HALF

    def one_hot(cells):
        return (lax.broadcasted_iota(jnp.int32, (C, C), 0) == cells).astype(F32).astype(BF16)

    def tables(kind, cols, first):
        place = cols - first
        own = jnp.where(low_lane, place[1:2], place[0:1])
        reach = jnp.where(low_lane, place[0:1], place[1:2])
        hot_near[kind] = one_hot(own)
        left = jnp.where(reach < 0, reach + HALF, -1)
        right = jnp.where(reach >= C, reach - HALF, -1)
        rim = jnp.maximum(left, right)
        swapped = jnp.where(rim < 0, rim, lax.rem(rim + HALF, C))
        hot_far[kind, 0] = one_hot(rim)
        hot_far[kind, 1] = one_hot(swapped)
        hot_far[kind, 2] = one_hot(reach)

    field[...] = jnp.zeros_like(field)

    def clear(kind, k):
        for rim in range(len(RIM_KINDS)):
            if RIM_KINDS[rim] == kind:
                get_rim[rim, :, k] = jnp.zeros((GROUPS, SPAN, C), BF16)

    for kind in (FINE, COARSE):
        for k in range(2):
            pl.when(~beyond[kind][1 - k])(functools.partial(clear, kind, k))

    def widen_diag(kind, start, stop):
        sub = lax.broadcasted_iota(jnp.int32, (8, C), 0)

        def step(block, carry):
            low = pl.multiple_of(block * 8, 8)
            total = jnp.zeros((8, C), F32)
            for i in range(8):
                diag[kind, low + i] = diag_in[kind, low + i].astype(F32)
                total = jnp.where(sub == i, diag[kind, low + i, pl.ds(low, 8), :], total)
            scale[kind, pl.ds(low, 8), :] = 1.0 / total
            return carry

        lax.fori_loop(start // 8, stop // 8, step, 0)

    def widen_off(target, first, start, stop):
        mask = lane_low(S)

        def step(block, carry):
            for i in range(4):
                row = start + block * 4 + i
                target[row] = jnp.where(mask, off_in[row, first], off_in[row, 1 - first]).astype(F32)
            return carry

        lax.fori_loop(0, (stop - start) // 4, step, 0)

    def smooth(kind, group, scaled=False):
        if not scaled:
            for r in range(PAIR):
                u[r] = q[group, r] * scale[kind]

        def step(block, carry):
            base = block * 8
            sums = products(
                [
                    (
                        lambda i, low: diag[kind, base + i, low : low + 8, :],
                        lambda r, low: u[r, low : low + 8, :],
                    )
                ]
            )
            rows = pl.ds(pl.multiple_of(base, 8), 8)
            for r in range(PAIR):
                total = fold_rows([sums[i][r] for i in range(8)])
                change = (OMEGA * scale[kind, rows, :]) * (2.0 * q[group, r, rows, :] - total)
                field[kind, group, r, rows, :] = field[kind, group, r, rows, :] + change
            return carry

        lax.fori_loop(0, S // 8, step, 0, unroll=2)

    def start_rims(rim, group, kind):
        whole = field[kind, group].reshape(PAIR * S, C)
        lower = pltpu.roll(whole[:SPAN], HALF, 1)
        upper = whole[SPAN:]
        mask = lane_low(SPAN)
        send_rim[rim, group, 0] = jnp.where(mask, lower, upper).astype(BF16)
        send_rim[rim, group, 1] = jnp.where(mask, upper, lower).astype(BF16)
        for k, copy in enumerate(rim_copies(rim, group, kind)):
            pl.when(beyond[kind][k])(copy.start)

    def apply_near(group, kind):
        rounded = field[kind, group].astype(BF16)
        xb[group] = rounded.reshape(PAIR * S, C)
        xw[group] = rounded.astype(F32)
        near[...] = jnp.dot(xb[group], hot_near[kind], preferred_element_type=F32).reshape(PAIR, S, C)
        start, first, rows = (0, 0, S) if kind == FINE else (level * ROWS, S, ROWS)

        def step(block, carry):
            base = block * 8
            sums = products(
                [
                    (
                        lambda i, low: diag[kind, start + base + i, low : low + 8, :],
                        lambda r, low: xw[group, r, low : low + 8, :],
                    ),
                    (
                        lambda i, low: off_near[first + base + i, low : low + 8, :],
                        lambda r, low: near[r, low : low + 8, :],
                    ),
                ]
            )
            if kind == FINE:
                for i in range(8):
                    for r in range(PAIR):
                        acc[group, block, i * PAIR + r] = sums[i][r]
                return carry
            place = pl.ds(pl.multiple_of(start + base, 8), 8)
            for r in range(PAIR):
                total = fold_rows([sums[i][r] for i in range(8)])
                q[group, r, place, :] = fixed[kind, group, r, place, :] - total
            return carry

        lax.fori_loop(0, rows // 8, step, 0, unroll=2)

    def gather_own(group, kind):
        far[group] = jnp.dot(xb[group], hot_far[kind, 2], preferred_element_type=F32)

    def finish_rims(rim, group, kind):
        for k, copy in enumerate(rim_copies(rim, group, kind)):
            pl.when(beyond[kind][1 - k])(copy.wait_recv)
        left = get_rim[rim, group, 0]
        right = get_rim[rim, group, 1]
        mask = lane_low(SPAN)
        for k in range(2):
            own = slice(k * SPAN, (k + 1) * SPAN)
            ends = jnp.where(mask, left, right) if k == 0 else jnp.where(mask, right, left)
            far[group, own] = far[group, own] + jnp.dot(
                ends, hot_far[kind, k], preferred_element_type=F32
            )
        first = 0 if kind == FINE else S

        def step(block, carry):
            base = block * 8
            held = None
            if kind == FINE:
                held = [[acc[group, block, i * PAIR + r] for r in range(PAIR)] for i in range(8)]
            sums = products(
                [
                    (
                        lambda i, low: off_far[first + base + i, low : low + 8, :],
                        lambda r, low: far[group, r * S + low : r * S + low + 8],
                    )
                ],
                held,
            )
            rows = pl.ds(pl.multiple_of(base, 8), 8)
            for r in range(PAIR):
                total = fold_rows([sums[i][r] for i in range(8)])
                known = fixed[kind, group, r, rows, :] if kind == FINE else q[group, r, rows, :]
                value = known - total
                q[group, r, rows, :] = value
                u[r, rows, :] = value * scale[kind, rows, :]
            return carry

        lax.fori_loop(0, S // 8, step, 0, unroll=2)

    def split_dot(value, dims):
        high = value.astype(BF16)
        low = (value - high.astype(F32)).astype(BF16)
        return sum(
            lax.dot_general(part, member[...], (dims, ((), ())), preferred_element_type=F32)
            for part in (high, low)
        )

    own_rows = pl.ds(pl.multiple_of(level * ROWS, ROWS), ROWS)

    def send_residual(group):
        part = split_dot(q[group].reshape(PAIR * S, C), ((1,), (1,)))
        send_part[group] = part.astype(BF16)
        for k in far_first:
            part_copies(group)[k].start()

    def sum_residual(group):
        for copy in part_copies(group):
            copy.wait_recv()
        total = send_part[group].astype(F32)
        for k in range(levels - 1):
            total = total + get_part[group, k].astype(F32)
        fixed[COARSE, group] = total.reshape(PAIR, S, C)
        q[group] = total.reshape(PAIR, S, C)

    def send_shortfall(sweep, group):
        for r in range(PAIR):
            value = q[group, r, own_rows, :].astype(BF16)
            send_short[sweep, group, r] = value
            q[group, r, own_rows, :] = value.astype(F32)
        for k in far_first:
            short_copies(sweep, group)[k].start()

    def join_shortfall(sweep, group):
        for k, copy in enumerate(short_copies(sweep, group)):
            copy.wait_recv()
            rows = pl.ds(source_rows(k), ROWS)
            for r in range(PAIR):
                q[group, r, rows, :] = get_short[sweep, group, k, r].astype(F32)

    def pick_far():
        mask = lane_low(S)

        def step(row, carry):
            send_far[row] = jnp.where(mask, off_in[S + row, 0], off_in[S + row, 1])
            return carry

        lax.fori_loop(0, ROWS, step, 0, unroll=4)

    def join_far():
        for piece in range(ROWS // PIECE):
            for copy in far_copies(piece):
                copy.wait_recv()

        def step(block, carry):
            for i in range(4):
                row = block * 4 + i
                off_far[S + level * ROWS + row] = send_far[row].astype(F32)
                for k in range(levels - 1):
                    off_far[source_rows(k, S) + row] = get_far[k, row].astype(F32)
            return carry

        lax.fori_loop(0, ROWS // 4, step, 0)

    groups = range(GROUPS)

    def save(group):
        own = slice(group * PAIR, (group + 1) * PAIR)
        return pltpu.make_async_copy(field.at[FINE, group], out_hbm.at[own], save_sem.at[group])

    for k in range(2):
        load_diag[k].wait()
        widen_diag(FINE, k * half, (k + 1) * half)
    load_rhs.wait()
    for r in range(R):
        value = rhs_in[:, r, :]
        fixed[FINE, r // PAIR, r % PAIR] = value
        q[r // PAIR, r % PAIR] = value
    for group in groups:
        smooth(FINE, group)
        if group == 0:
            pl.semaphore_wait(barrier, awaited)
        start_rims(0, group, FINE)
    load_coff.wait()
    pick_far()
    start_far(0)
    load_cols.wait()
    tables(FINE, cols_ref[...], index * C)
    for k in range(2):
        load_off[k].wait()
        widen_off(off_near, 1, k * half, (k + 1) * half)
    for group in groups:
        apply_near(group, FINE)
        gather_own(group, FINE)
    widen_off(off_far, 0, 0, S)
    for copy in load_coarse:
        copy.wait()
    member[...] = one_hot(agg_ref[...] - space * C)
    for group in groups:
        finish_rims(0, group, FINE)
        smooth(FINE, group, scaled=True)
        start_rims(1, group, FINE)
    start_far(1)
    for group in groups:
        apply_near(group, FINE)
        gather_own(group, FINE)
    for group in groups:
        finish_rims(1, group, FINE)
        send_residual(group)
    start_far(2)
    start_far(3)
    tables(COARSE, ccols_ref[...], space * C)
    widen_diag(COARSE, 0, S)
    widen_off(off_near, 1, S, S + ROWS)
    for group in groups:
        sum_residual(group)
        smooth(COARSE, group)
        start_rims(2, group, COARSE)
        apply_near(group, COARSE)
        send_shortfall(0, group)
    for group in groups:
        gather_own(group, COARSE)
    join_far()
    for group in groups:
        join_shortfall(0, group)
        finish_rims(2, group, COARSE)
        smooth(COARSE, group, scaled=True)
        start_rims(3, group, COARSE)
        apply_near(group, COARSE)
        send_shortfall(1, group)
    for group in groups:
        gather_own(group, COARSE)
    for group in groups:
        join_shortfall(1, group)
        finish_rims(3, group, COARSE)
        smooth(COARSE, group, scaled=True)
        spread = split_dot(field[COARSE, group].reshape(PAIR * S, C), ((1,), (0,)))
        field[FINE, group] = field[FINE, group] + spread.reshape(PAIR, S, C)
        start_rims(4, group, FINE)
    for group in groups:
        apply_near(group, FINE)
        gather_own(group, FINE)
    for group in groups:
        finish_rims(4, group, FINE)
        smooth(FINE, group, scaled=True)
        save(group).start()
    for piece in range(ROWS // PIECE):
        for copy in far_copies(piece):
            copy.wait_send()
    for group in groups:
        save(group).wait()
        for rim in range(len(RIM_KINDS)):
            kind = RIM_KINDS[rim]
            for k, copy in enumerate(rim_copies(rim, group, kind)):
                pl.when(beyond[kind][k])(copy.wait_send)
        for copy in part_copies(group):
            copy.wait_send()
        for sweep in range(2):
            for copy in short_copies(sweep, group):
                copy.wait_send()


def local(sizes, rhs, fine_diag, fine_off, fine_cols, aggregates, coarse_diag, coarse_off, coarse_cols):
    others = sizes[1] - 1
    hbm = pl.BlockSpec(memory_space=pl.ANY)
    dma = pltpu.SemaphoreType.DMA
    result = pl.pallas_call(
        functools.partial(kernel, sizes),
        out_shape=jax.ShapeDtypeStruct((R, S, C), F32),
        in_specs=[hbm] * 8,
        out_specs=hbm,
        scratch_shapes=[
            pltpu.VMEM((2, C), jnp.int32),
            pltpu.VMEM((1, C), jnp.int32),
            pltpu.VMEM((2, C), jnp.int32),
            pltpu.VMEM((S, R, C), F32),
            pltpu.VMEM((2, S, S, C), BF16),
            pltpu.VMEM((S + ROWS, 2, S, C), BF16),
            pltpu.VMEM((2, S, S, C), F32),
            pltpu.VMEM((S + ROWS, S, C), F32),
            pltpu.VMEM((2 * S, S, C), F32),
            pltpu.VMEM((2, S, C), F32),
            pltpu.VMEM((2, GROUPS, PAIR, S, C), F32),
            pltpu.VMEM((2, GROUPS, PAIR, S, C), F32),
            pltpu.VMEM((GROUPS, PAIR, S, C), F32),
            pltpu.VMEM((PAIR, S, C), F32),
            pltpu.VMEM((GROUPS, PAIR * S, C), BF16),
            pltpu.VMEM((GROUPS, PAIR, S, C), F32),
            pltpu.VMEM((PAIR, S, C), F32),
            pltpu.VMEM((GROUPS, PAIR * S, C), F32),
            pltpu.VMEM((GROUPS, S // 8, 8 * PAIR, 8, C), F32),
            pltpu.VMEM((2, C, C), BF16),
            pltpu.VMEM((2, 3, C, C), BF16),
            pltpu.VMEM((C, C), BF16),
            pltpu.VMEM((len(RIM_KINDS), GROUPS, 2, SPAN, C), BF16),
            pltpu.VMEM((len(RIM_KINDS), GROUPS, 2, SPAN, C), BF16),
            pltpu.VMEM((GROUPS, PAIR * S, C), BF16),
            pltpu.VMEM((GROUPS, others, PAIR * S, C), BF16),
            pltpu.VMEM((2, GROUPS, PAIR, ROWS, C), BF16),
            pltpu.VMEM((2, GROUPS, others, PAIR, ROWS, C), BF16),
            pltpu.VMEM((ROWS, S, C), BF16),
            pltpu.VMEM((others, ROWS, S, C), BF16),
            dma((10,)),
            dma((GROUPS,)),
            dma((len(RIM_KINDS), GROUPS, 2)),
            dma((len(RIM_KINDS), GROUPS, 2)),
            dma((GROUPS, others)),
            dma((GROUPS, others)),
            dma((2, GROUPS, others)),
            dma((2, GROUPS, others)),
            dma((ROWS // PIECE, others)),
            dma((ROWS // PIECE, others)),
        ],
        compiler_params=pltpu.CompilerParams(
            collective_id=0, has_side_effects=True, vmem_limit_bytes=63 * 1024 * 1024
        ),
        name="vcycle",
    )(
        rhs, fine_diag, fine_off, fine_cols, aggregates.reshape(1, C),
        coarse_diag, coarse_off, coarse_cols,
    )
    return result.transpose(1, 0, 2)


def solution(mesh):
    placed = (
        P(None, None, ("space", "level")),
        P(None, None, ("space", "level")),
        P(None, None, None, ("space", "level")),
        P(None, ("space", "level")),
        P(("space", "level")),
        P(None, None, "space"),
        P("level", None, None, "space"),
        P(None, "space"),
    )
    sizes = (mesh.shape["space"], mesh.shape["level"])
    return jax.shard_map(
        functools.partial(local, sizes),
        mesh=mesh,
        in_specs=placed,
        out_specs=P(None, None, ("space", "level")),
        check_vma=False,
    )
```

```python
import functools

import jax
import jax.numpy as jnp
from jax import lax
from jax.experimental import pallas as pl
from jax.experimental.pallas import tpu as pltpu
from jax.sharding import PartitionSpec as P

OMEGA = 0.7
S = 64
R = 4
GROUPS = 2
PAIR = R // GROUPS
C = 128
HALF = 64
ROWS = 16
PIECE = 4
SPAN = PAIR * S // 2
FINE, COARSE = 0, 1
RIM_KINDS = (FINE, FINE, COARSE, COARSE, FINE)
MESH = pl.DeviceIdType.MESH
F32 = jnp.float32
BF16 = jnp.bfloat16


def lane_low(rows):
    return lax.broadcasted_iota(jnp.int32, (rows, C), 1) < HALF


def fold_rows(parts):
    sub = lax.broadcasted_iota(jnp.int32, (8, C), 0)
    four = sub < 4
    two = lax.rem(sub, 4) < 2
    one = lax.rem(sub, 2) < 1
    level = [
        jnp.where(four, parts[i], parts[i + 4])
        + pltpu.roll(jnp.where(four, parts[i + 4], parts[i]), 4, 0)
        for i in range(4)
    ]
    level = [
        jnp.where(
            two,
            level[i] + pltpu.roll(level[i], 6, 0),
            level[i + 2] + pltpu.roll(level[i + 2], 2, 0),
        )
        for i in range(2)
    ]
    return jnp.where(
        one,
        level[0] + pltpu.roll(level[0], 7, 0),
        level[1] + pltpu.roll(level[1], 1, 0),
    )


def products(terms, start=None):
    sums = [[None] * PAIR for _ in range(8)] if start is None else start
    for load, vector in terms:
        for low in range(0, S, 8):
            pieces = [vector(r, low) for r in range(PAIR)]
            for i in range(8):
                matrix = load(i, low)
                for r in range(PAIR):
                    piece = matrix * pieces[r]
                    sums[i][r] = piece if sums[i][r] is None else sums[i][r] + piece
    return sums


def kernel(
    sizes,
    rhs_hbm, diag_hbm, off_hbm, cols_hbm, agg_hbm, cdiag_hbm, coff_hbm, ccols_hbm,
    out_hbm,
    cols_ref, agg_ref, ccols_ref, rhs_in, diag_in, off_in, diag, off_near, off_far, scale, fixed, field, q, u, xb, xw, near, far, acc,
    hot_near, hot_far, member,
    send_rim, get_rim, send_part, get_part, send_short, get_short, send_far, get_far,
    load_sem, save_sem, rim_send, rim_get, part_send, part_get, short_send, short_get, far_send, far_get,
):
    spaces, levels = sizes
    space = lax.axis_index("space")
    level = lax.axis_index("level")
    index = space * levels + level
    count = spaces * levels
    after = lax.rem(index + 1, count)
    before = lax.rem(index + count - 1, count)
    fine_next = (lax.div(after, levels), lax.rem(after, levels))
    fine_last = (lax.div(before, levels), lax.rem(before, levels))
    space_next = (lax.rem(space + 1, spaces), level)
    space_last = (lax.rem(space + spaces - 1, spaces), level)
    peers = [(space, lax.rem(level + k, levels)) for k in range(1, levels)]

    beyond = {
        FINE: (index < count - 1, index > 0),
        COARSE: (space < spaces - 1, space > 0),
    }
    targets = {FINE: (fine_next, fine_last), COARSE: (space_next, space_last)}

    far_first = sorted(range(levels - 1), key=lambda k: -min(k + 1, levels - 1 - k))

    barrier = pltpu.get_barrier_semaphore()
    awaited = levels - 1

    def greet(partner):
        pl.semaphore_signal(barrier, inc=1, device_id=partner, device_id_type=MESH)

    for partner in peers:
        greet(partner)
    for kind in (FINE, COARSE):
        for k in range(2):
            awaited = awaited + beyond[kind][k].astype(jnp.int32)
            pl.when(beyond[kind][k])(functools.partial(greet, targets[kind][k]))

    def load(k, source, target):
        return pltpu.make_async_copy(source, target, load_sem.at[k])

    half = S // 2
    load_diag = [
        load(k, diag_hbm.at[k * half : (k + 1) * half], diag_in.at[FINE, k * half : (k + 1) * half])
        for k in range(2)
    ]
    load_rhs = load(2, rhs_hbm, rhs_in)
    load_cols = load(3, cols_hbm, cols_ref)
    load_off = [
        load(4 + k, off_hbm.at[k * half : (k + 1) * half], off_in.at[k * half : (k + 1) * half])
        for k in range(2)
    ]
    load_coff = load(9, coff_hbm, off_in.at[S : S + ROWS])
    load_coarse = [
        load(6, agg_hbm, agg_ref),
        load(7, ccols_hbm, ccols_ref),
        load(8, cdiag_hbm, diag_in.at[COARSE]),
    ]
    for copy in load_diag + [load_rhs, load_coff, load_cols] + load_off + load_coarse:
        copy.start()

    def remote(source, target, sent, got, device):
        return pltpu.make_async_remote_copy(
            src_ref=source, dst_ref=target, send_sem=sent, recv_sem=got,
            device_id=device, device_id_type=MESH,
        )

    def rim_copies(rim, group, kind):
        return [
            remote(
                send_rim.at[rim, group, k], get_rim.at[rim, group, k],
                rim_send.at[rim, group, k], rim_get.at[rim, group, k], targets[kind][k],
            )
            for k in range(2)
        ]

    def part_copies(group):
        return [
            remote(
                send_part.at[group], get_part.at[group, k],
                part_send.at[group, k], part_get.at[group, k], peer,
            )
            for k, peer in enumerate(peers)
        ]

    def short_copies(sweep, group):
        return [
            remote(
                send_short.at[sweep, group], get_short.at[sweep, group, k],
                short_send.at[sweep, group, k], short_get.at[sweep, group, k], peer,
            )
            for k, peer in enumerate(peers)
        ]

    def far_copies(piece):
        rows = slice(piece * PIECE, (piece + 1) * PIECE)
        return [
            remote(
                send_far.at[rows], get_far.at[k, rows],
                far_send.at[piece, k], far_get.at[piece, k], peer,
            )
            for k, peer in enumerate(peers)
        ]

    def start_far(piece):
        for k in far_first:
            far_copies(piece)[k].start()

    def source_rows(k, first=0):
        source = lax.rem(level + levels - (k + 1), levels)
        return first + pl.multiple_of(source * ROWS, ROWS)

    low_lane = lax.broadcasted_iota(jnp.int32, (1, C), 1) < HALF

    def one_hot(cells):
        return (lax.broadcasted_iota(jnp.int32, (C, C), 0) == cells).astype(F32).astype(BF16)

    def tables(kind, cols, first):
        place = cols - first
        own = jnp.where(low_lane, place[1:2], place[0:1])
        reach = jnp.where(low_lane, place[0:1], place[1:2])
        hot_near[kind] = one_hot(own)
        left = jnp.where(reach < 0, reach + HALF, -1)
        right = jnp.where(reach >= C, reach - HALF, -1)
        rim = jnp.maximum(left, right)
        swapped = jnp.where(rim < 0, rim, lax.rem(rim + HALF, C))
        hot_far[kind, 0] = one_hot(rim)
        hot_far[kind, 1] = one_hot(swapped)
        hot_far[kind, 2] = one_hot(reach)

    field[...] = jnp.zeros_like(field)

    def clear(kind, k):
        for rim in range(len(RIM_KINDS)):
            if RIM_KINDS[rim] == kind:
                get_rim[rim, :, k] = jnp.zeros((GROUPS, SPAN, C), BF16)

    for kind in (FINE, COARSE):
        for k in range(2):
            pl.when(~beyond[kind][1 - k])(functools.partial(clear, kind, k))

    def widen_diag(kind, start, stop):
        sub = lax.broadcasted_iota(jnp.int32, (8, C), 0)

        def step(block, carry):
            low = pl.multiple_of(block * 8, 8)
            total = jnp.zeros((8, C), F32)
            for i in range(8):
                diag[kind, low + i] = diag_in[kind, low + i].astype(F32)
                total = jnp.where(sub == i, diag[kind, low + i, pl.ds(low, 8), :], total)
            scale[kind, pl.ds(low, 8), :] = 1.0 / total
            return carry

        lax.fori_loop(start // 8, stop // 8, step, 0)

    def widen_off(target, first, start, stop):
        mask = lane_low(S)

        def step(block, carry):
            for i in range(4):
                row = start + block * 4 + i
                target[row] = jnp.where(mask, off_in[row, first], off_in[row, 1 - first]).astype(F32)
            return carry

        lax.fori_loop(0, (stop - start) // 4, step, 0)

    def smooth(kind, group, scaled=False):
        if not scaled:
            for r in range(PAIR):
                u[r] = q[group, r] * scale[kind]

        def step(block, carry):
            base = block * 8
            sums = products(
                [
                    (
                        lambda i, low: diag[kind, base + i, low : low + 8, :],
                        lambda r, low: u[r, low : low + 8, :],
                    )
                ]
            )
            rows = pl.ds(pl.multiple_of(base, 8), 8)
            for r in range(PAIR):
                total = fold_rows([sums[i][r] for i in range(8)])
                change = (OMEGA * scale[kind, rows, :]) * (2.0 * q[group, r, rows, :] - total)
                field[kind, group, r, rows, :] = field[kind, group, r, rows, :] + change
            return carry

        lax.fori_loop(0, S // 8, step, 0, unroll=4)

    def start_rims(rim, group, kind):
        whole = field[kind, group].reshape(PAIR * S, C)
        lower = pltpu.roll(whole[:SPAN], HALF, 1)
        upper = whole[SPAN:]
        mask = lane_low(SPAN)
        send_rim[rim, group, 0] = jnp.where(mask, lower, upper).astype(BF16)
        send_rim[rim, group, 1] = jnp.where(mask, upper, lower).astype(BF16)
        for k, copy in enumerate(rim_copies(rim, group, kind)):
            pl.when(beyond[kind][k])(copy.start)

    def apply_near(group, kind):
        rounded = field[kind, group].astype(BF16)
        xb[group] = rounded.reshape(PAIR * S, C)
        xw[group] = rounded.astype(F32)
        near[...] = jnp.dot(xb[group], hot_near[kind], preferred_element_type=F32).reshape(PAIR, S, C)
        start, first, rows = (0, 0, S) if kind == FINE else (level * ROWS, S, ROWS)

        def step(block, carry):
            base = block * 8
            sums = products(
                [
                    (
                        lambda i, low: diag[kind, start + base + i, low : low + 8, :],
                        lambda r, low: xw[group, r, low : low + 8, :],
                    ),
                    (
                        lambda i, low: off_near[first + base + i, low : low + 8, :],
                        lambda r, low: near[r, low : low + 8, :],
                    ),
                ]
            )
            if kind == FINE:
                for i in range(8):
                    for r in range(PAIR):
                        acc[group, block, i * PAIR + r] = sums[i][r]
                return carry
            place = pl.ds(pl.multiple_of(start + base, 8), 8)
            for r in range(PAIR):
                total = fold_rows([sums[i][r] for i in range(8)])
                q[group, r, place, :] = fixed[kind, group, r, place, :] - total
            return carry

        lax.fori_loop(0, rows // 8, step, 0, unroll=2)

    def gather_own(group, kind):
        far[group] = jnp.dot(xb[group], hot_far[kind, 2], preferred_element_type=F32)

    def finish_rims(rim, group, kind):
        for k, copy in enumerate(rim_copies(rim, group, kind)):
            pl.when(beyond[kind][1 - k])(copy.wait_recv)
        left = get_rim[rim, group, 0]
        right = get_rim[rim, group, 1]
        mask = lane_low(SPAN)
        for k in range(2):
            own = slice(k * SPAN, (k + 1) * SPAN)
            ends = jnp.where(mask, left, right) if k == 0 else jnp.where(mask, right, left)
            far[group, own] = far[group, own] + jnp.dot(
                ends, hot_far[kind, k], preferred_element_type=F32
            )
        first = 0 if kind == FINE else S

        def step(block, carry):
            base = block * 8
            held = None
            if kind == FINE:
                held = [[acc[group, block, i * PAIR + r] for r in range(PAIR)] for i in range(8)]
            sums = products(
                [
                    (
                        lambda i, low: off_far[first + base + i, low : low + 8, :],
                        lambda r, low: far[group, r * S + low : r * S + low + 8],
                    )
                ],
                held,
            )
            rows = pl.ds(pl.multiple_of(base, 8), 8)
            for r in range(PAIR):
                total = fold_rows([sums[i][r] for i in range(8)])
                known = fixed[kind, group, r, rows, :] if kind == FINE else q[group, r, rows, :]
                value = known - total
                q[group, r, rows, :] = value
                u[r, rows, :] = value * scale[kind, rows, :]
            return carry

        lax.fori_loop(0, S // 8, step, 0, unroll=4)

    def split_dot(value, dims):
        high = value.astype(BF16)
        low = (value - high.astype(F32)).astype(BF16)
        return sum(
            lax.dot_general(part, member[...], (dims, ((), ())), preferred_element_type=F32)
            for part in (high, low)
        )

    own_rows = pl.ds(pl.multiple_of(level * ROWS, ROWS), ROWS)

    def send_residual(group):
        part = split_dot(q[group].reshape(PAIR * S, C), ((1,), (1,)))
        send_part[group] = part.astype(BF16)
        for k in far_first:
            part_copies(group)[k].start()

    def sum_residual(group):
        for copy in part_copies(group):
            copy.wait_recv()
        total = send_part[group].astype(F32)
        for k in range(levels - 1):
            total = total + get_part[group, k].astype(F32)
        fixed[COARSE, group] = total.reshape(PAIR, S, C)
        q[group] = total.reshape(PAIR, S, C)

    def send_shortfall(sweep, group):
        for r in range(PAIR):
            value = q[group, r, own_rows, :].astype(BF16)
            send_short[sweep, group, r] = value
            q[group, r, own_rows, :] = value.astype(F32)
        for k in far_first:
            short_copies(sweep, group)[k].start()

    def join_shortfall(sweep, group):
        for k, copy in enumerate(short_copies(sweep, group)):
            copy.wait_recv()
            rows = pl.ds(source_rows(k), ROWS)
            for r in range(PAIR):
                q[group, r, rows, :] = get_short[sweep, group, k, r].astype(F32)

    def pick_far():
        mask = lane_low(S)

        def step(row, carry):
            send_far[row] = jnp.where(mask, off_in[S + row, 0], off_in[S + row, 1])
            return carry

        lax.fori_loop(0, ROWS, step, 0, unroll=4)

    def join_far():
        for piece in range(ROWS // PIECE):
            for copy in far_copies(piece):
                copy.wait_recv()

        def step(block, carry):
            for i in range(4):
                row = block * 4 + i
                off_far[S + level * ROWS + row] = send_far[row].astype(F32)
                for k in range(levels - 1):
                    off_far[source_rows(k, S) + row] = get_far[k, row].astype(F32)
            return carry

        lax.fori_loop(0, ROWS // 4, step, 0)

    groups = range(GROUPS)

    def save(group):
        own = slice(group * PAIR, (group + 1) * PAIR)
        return pltpu.make_async_copy(field.at[FINE, group], out_hbm.at[own], save_sem.at[group])

    for k in range(2):
        load_diag[k].wait()
        widen_diag(FINE, k * half, (k + 1) * half)
    load_rhs.wait()
    for r in range(R):
        value = rhs_in[:, r, :]
        fixed[FINE, r // PAIR, r % PAIR] = value
        q[r // PAIR, r % PAIR] = value
    for group in groups:
        smooth(FINE, group)
        if group == 0:
            pl.semaphore_wait(barrier, awaited)
        start_rims(0, group, FINE)
    load_coff.wait()
    pick_far()
    start_far(0)
    load_cols.wait()
    tables(FINE, cols_ref[...], index * C)
    for k in range(2):
        load_off[k].wait()
        widen_off(off_near, 1, k * half, (k + 1) * half)
    for group in groups:
        apply_near(group, FINE)
        gather_own(group, FINE)
    widen_off(off_far, 0, 0, S)
    for copy in load_coarse:
        copy.wait()
    member[...] = one_hot(agg_ref[...] - space * C)
    for group in groups:
        finish_rims(0, group, FINE)
        smooth(FINE, group, scaled=True)
        start_rims(1, group, FINE)
    start_far(1)
    for group in groups:
        apply_near(group, FINE)
        gather_own(group, FINE)
    for group in groups:
        finish_rims(1, group, FINE)
        send_residual(group)
    start_far(2)
    start_far(3)
    tables(COARSE, ccols_ref[...], space * C)
    widen_diag(COARSE, 0, S)
    widen_off(off_near, 1, S, S + ROWS)
    for group in groups:
        sum_residual(group)
        smooth(COARSE, group)
        start_rims(2, group, COARSE)
        apply_near(group, COARSE)
        send_shortfall(0, group)
    for group in groups:
        gather_own(group, COARSE)
    join_far()
    for group in groups:
        join_shortfall(0, group)
        finish_rims(2, group, COARSE)
        smooth(COARSE, group, scaled=True)
        start_rims(3, group, COARSE)
        apply_near(group, COARSE)
        send_shortfall(1, group)
    for group in groups:
        gather_own(group, COARSE)
    for group in groups:
        join_shortfall(1, group)
        finish_rims(3, group, COARSE)
        smooth(COARSE, group, scaled=True)
        spread = split_dot(field[COARSE, group].reshape(PAIR * S, C), ((1,), (0,)))
        field[FINE, group] = field[FINE, group] + spread.reshape(PAIR, S, C)
        start_rims(4, group, FINE)
    for group in groups:
        apply_near(group, FINE)
        gather_own(group, FINE)
    for group in groups:
        finish_rims(4, group, FINE)
        smooth(FINE, group, scaled=True)
        save(group).start()
    for piece in range(ROWS // PIECE):
        for copy in far_copies(piece):
            copy.wait_send()
    for group in groups:
        save(group).wait()
        for rim in range(len(RIM_KINDS)):
            kind = RIM_KINDS[rim]
            for k, copy in enumerate(rim_copies(rim, group, kind)):
                pl.when(beyond[kind][k])(copy.wait_send)
        for copy in part_copies(group):
            copy.wait_send()
        for sweep in range(2):
            for copy in short_copies(sweep, group):
                copy.wait_send()


def local(sizes, rhs, fine_diag, fine_off, fine_cols, aggregates, coarse_diag, coarse_off, coarse_cols):
    others = sizes[1] - 1
    hbm = pl.BlockSpec(memory_space=pl.ANY)
    dma = pltpu.SemaphoreType.DMA
    result = pl.pallas_call(
        functools.partial(kernel, sizes),
        out_shape=jax.ShapeDtypeStruct((R, S, C), F32),
        in_specs=[hbm] * 8,
        out_specs=hbm,
        scratch_shapes=[
            pltpu.VMEM((2, C), jnp.int32),
            pltpu.VMEM((1, C), jnp.int32),
            pltpu.VMEM((2, C), jnp.int32),
            pltpu.VMEM((S, R, C), F32),
            pltpu.VMEM((2, S, S, C), BF16),
            pltpu.VMEM((S + ROWS, 2, S, C), BF16),
            pltpu.VMEM((2, S, S, C), F32),
            pltpu.VMEM((S + ROWS, S, C), F32),
            pltpu.VMEM((2 * S, S, C), F32),
            pltpu.VMEM((2, S, C), F32),
            pltpu.VMEM((2, GROUPS, PAIR, S, C), F32),
            pltpu.VMEM((2, GROUPS, PAIR, S, C), F32),
            pltpu.VMEM((GROUPS, PAIR, S, C), F32),
            pltpu.VMEM((PAIR, S, C), F32),
            pltpu.VMEM((GROUPS, PAIR * S, C), BF16),
            pltpu.VMEM((GROUPS, PAIR, S, C), F32),
            pltpu.VMEM((PAIR, S, C), F32),
            pltpu.VMEM((GROUPS, PAIR * S, C), F32),
            pltpu.VMEM((GROUPS, S // 8, 8 * PAIR, 8, C), F32),
            pltpu.VMEM((2, C, C), BF16),
            pltpu.VMEM((2, 3, C, C), BF16),
            pltpu.VMEM((C, C), BF16),
            pltpu.VMEM((len(RIM_KINDS), GROUPS, 2, SPAN, C), BF16),
            pltpu.VMEM((len(RIM_KINDS), GROUPS, 2, SPAN, C), BF16),
            pltpu.VMEM((GROUPS, PAIR * S, C), BF16),
            pltpu.VMEM((GROUPS, others, PAIR * S, C), BF16),
            pltpu.VMEM((2, GROUPS, PAIR, ROWS, C), BF16),
            pltpu.VMEM((2, GROUPS, others, PAIR, ROWS, C), BF16),
            pltpu.VMEM((ROWS, S, C), BF16),
            pltpu.VMEM((others, ROWS, S, C), BF16),
            dma((10,)),
            dma((GROUPS,)),
            dma((len(RIM_KINDS), GROUPS, 2)),
            dma((len(RIM_KINDS), GROUPS, 2)),
            dma((GROUPS, others)),
            dma((GROUPS, others)),
            dma((2, GROUPS, others)),
            dma((2, GROUPS, others)),
            dma((ROWS // PIECE, others)),
            dma((ROWS // PIECE, others)),
        ],
        compiler_params=pltpu.CompilerParams(
            collective_id=0, has_side_effects=True, vmem_limit_bytes=63 * 1024 * 1024
        ),
        name="vcycle",
    )(
        rhs, fine_diag, fine_off, fine_cols, aggregates.reshape(1, C),
        coarse_diag, coarse_off, coarse_cols,
    )
    return result.transpose(1, 0, 2)


def solution(mesh):
    placed = (
        P(None, None, ("space", "level")),
        P(None, None, ("space", "level")),
        P(None, None, None, ("space", "level")),
        P(None, ("space", "level")),
        P(("space", "level")),
        P(None, None, "space"),
        P("level", None, None, "space"),
        P(None, "space"),
    )
    sizes = (mesh.shape["space"], mesh.shape["level"])
    return jax.shard_map(
        functools.partial(local, sizes),
        mesh=mesh,
        in_specs=placed,
        out_specs=P(None, None, ("space", "level")),
        check_vma=False,
    )
```
